256 devices in a mesh: dp: 8 (over x, core), segment: 2 (over y_hi), blk: 16 (over y_lo, z).
Axes of the slice: x: 4, y: 4 (y_hi: 2, y_lo: 2; y = y_hi * 2 + y_lo), z: 8, core: 2. Of those that a mesh axis runs over, the one named last changes fastest.
Arguments:
- tokens: bfloat16 [8, 6144, 1280], P('dp', 'blk'), may hold values from -6 to 6
- targets: bfloat16 [8, 6144, 1176], P('dp', 'blk'), may hold values from -6 to 6
- visible: int32 [8, 6144], P('dp', 'blk'), may hold values from 0 to 1, as said below
- w_qkv: bfloat16 [1280, 1920], replicated, as said below
- w_out: bfloat16 [640, 1280], replicated, may hold values from -0.25 to 0.25
- w_embed: bfloat16 [1280, 512], replicated, may hold values from -0.15625 to 0.15625
- mask_token: bfloat16 [512], replicated, may hold values from -4 to 4
- dec_pos: bfloat16 [6144, 512], P('blk'), may hold values from -4 to 4
- w_up: bfloat16 [512, 1024], replicated, may hold values from -0.25 to 0.25
- w_down: bfloat16 [1024, 512], replicated, may hold values from -0.1875 to 0.1875
- w_head: bfloat16 [512, 1176], replicated, may hold values from -0.25 to 0.25
Outputs:
- grad_w_out: float32 [640, 1280], P('blk', ('dp', 'segment'))
- grad_w_up: float32 [512, 1024], P('blk', ('dp', 'segment'))
- grad_w_down: float32 [1024, 512], P('blk', ('dp', 'segment'))
The draws below stay inside these ranges and needn't reach their ends.
Inputs may be any that keep to these rules, and one draw needn't show every extreme that they name: In each scene every tile of 384 consecutive patches has at most 168 visible patches and one tile exactly 168; each scene has 1536 visible patches. `w_qkv`: the query, key and value projections side by side, 640 columns each.
All inputs are finite; a program needn't handle non-finite values.
Results may differ from the reference program's by a relative error of at most 0.018.
Values may be sent and summed in bfloat16 or wider, within the bound.
A program may use at most 128 MiB of HBM per device.

```python
import math
import jax
import jax.numpy as jnp
from jax import lax

D = 1280
HEADS = 8
HEAD_DIM = 80
DEC_WIDTH = 512
FF = 1024
PATCH_PIXELS = 1176
VIS_TILE = 96
TILE = 384
TILE_CAP = 168
INNER = 640
SCENES = 8
PATCHES = 6144
MASKED = 36864
N_BLK = 16


def tile_counts(count_key):
    key_big, key_order, key_amount = jax.random.split(count_key, 3)
    extra_rows = TILE_CAP - VIS_TILE
    other_count = N_BLK - 1
    base_loss = extra_rows // other_count
    spare_count = extra_rows % other_count
    pair_count = max(other_count // 2, 1)
    reach_top = max(1, (VIS_TILE - base_loss - 1) // 2)
    big_tile = jax.random.randint(key_big, (), 0, N_BLK)
    rank_order = jax.random.permutation(key_order, other_count)
    amount = jax.random.randint(key_amount, (pair_count,), 0, reach_top)
    tile_loss = base_loss + (rank_order < spare_count).astype(jnp.int32)
    pair_sign = jnp.where(rank_order % 2 == 0, 1, -1)
    pair_shift = jnp.where(rank_order < 2 * (other_count // 2), pair_sign * amount[jnp.minimum(rank_order // 2, pair_count - 1)], 0)
    other_values = VIS_TILE - tile_loss + pair_shift
    tile_index = jnp.arange(N_BLK)
    lookup = jnp.clip(tile_index - (tile_index > big_tile).astype(jnp.int32), 0, other_count - 1)
    return jnp.where(tile_index == big_tile, TILE_CAP, other_values[lookup]).astype(jnp.int32)


def draw_visible(key, part):
    key = jax.random.fold_in(key, 5)

    def one_scene(scene_key):
        key_count, key_place = jax.random.split(scene_key)
        counts = tile_counts(key_count)
        place_keys = jax.random.split(key_place, N_BLK)
        ranks = jax.vmap(lambda tile_key: jax.random.permutation(tile_key, TILE))(place_keys)
        return (ranks < counts[:, None]).astype(jnp.int32).reshape(PATCHES)
    return jax.vmap(one_scene)(jax.random.split(key, SCENES))


def draw_w_qkv(key, part):
    key = jax.random.fold_in(key, 11)
    key_query, key_key, key_value = jax.random.split(key, 3)
    spread = D ** (-0.5)
    query_part = jax.random.normal(key_query, (D, INNER), jnp.float32) * spread
    value_part = jax.random.normal(key_value, (D, INNER), jnp.float32) * spread
    key_part = jax.random.normal(key_key, (D, INNER), jnp.float32) * spread
    return jnp.concatenate([query_part, key_part, value_part], axis=1).astype(jnp.bfloat16)


def block_levels(key, dims, cuts, least, high):
    def one(dim, blocks):
        draws = jax.random.uniform(jax.random.fold_in(jax.random.fold_in(key, 6), dim), (blocks,), jnp.float32, least / len(cuts), high / len(cuts))
        return jnp.repeat(jnp.exp(draws), dims[dim] // blocks).reshape((-1,) + (1,) * (len(dims) - dim - 1))

    factor_of = one(*cuts[0])
    for cut in cuts[1:]:
        factor_of = factor_of * one(*cut)
    return factor_of


def noise(own_key, shape, width, limit, shards=(), kind=jnp.bfloat16):
    result = jax.random.normal(own_key, shape, jnp.float32) * width
    if len(shards) > 0:
        result = block_levels(own_key, shape, shards, -0.22, 0.18) * result
    return jnp.clip(result, min=-limit, max=limit).astype(kind)


def setup_inputs(seed: int = 0) -> dict:
    streams_of = jax.random.split(jax.random.key(seed), 12)
    return {
        "tokens": noise(streams_of[0], (SCENES, PATCHES, D), 1.0, 6.0, ((0, 8), (1, 16))),
        "targets": noise(streams_of[1], (SCENES, PATCHES, PATCH_PIXELS), 1.0, 6.0, ((0, 8), (1, 16))),
        "visible": draw_visible(jax.random.fold_in(streams_of[11], 71), 0),
        "w_qkv": draw_w_qkv(jax.random.fold_in(streams_of[11], 71), 0),
        "w_out": noise(streams_of[4], (INNER, D), INNER ** -0.5, 0.25),
        "w_embed": noise(streams_of[5], (D, DEC_WIDTH), D ** -0.5, 0.15625),
        "mask_token": noise(streams_of[6], (DEC_WIDTH,), 1.0, 4.0),
        "dec_pos": noise(streams_of[7], (PATCHES, DEC_WIDTH), 1.0, 4.0, ((0, 16),)),
        "w_up": noise(streams_of[8], (DEC_WIDTH, FF), DEC_WIDTH ** -0.5, 0.25),
        "w_down": noise(streams_of[9], (FF, DEC_WIDTH), FF ** -0.5, 0.1875),
        "w_head": noise(streams_of[10], (DEC_WIDTH, PATCH_PIXELS), DEC_WIDTH ** -0.5, 0.25),
    }


epsilon = 1e-05

def layer_norm(matrix):
    center = matrix - lax.optimization_barrier(jnp.mean(matrix, axis=-1, keepdims=True))
    return center * lax.rsqrt(lax.optimization_barrier(jnp.mean(center * center, axis=-1, keepdims=True)) + epsilon)

def norm_backward(matrix, gradient):
    center = matrix - lax.optimization_barrier(jnp.mean(matrix, axis=-1, keepdims=True))
    inverse = lax.rsqrt(lax.optimization_barrier(jnp.mean(center * center, axis=-1, keepdims=True)) + epsilon)
    normal_rows = center * inverse
    cross_mean = lax.optimization_barrier(jnp.mean(gradient * normal_rows, axis=-1, keepdims=True))
    return inverse * (gradient - lax.optimization_barrier(jnp.mean(gradient, axis=-1, keepdims=True)) - normal_rows * cross_mean)

def gelu_exact(inputs):
    return 0.5 * inputs * (1.0 + lax.erf(inputs * (1.0 / math.sqrt(2.0))))

def gelu_slope(inputs):
    cumulative = 0.5 * (1.0 + lax.erf(inputs * (1.0 / math.sqrt(2.0))))
    return cumulative + inputs * jnp.exp(-0.5 * inputs * inputs) * (1.0 / math.sqrt(2.0 * math.pi))

def slot_table(tile_seen, slot_count):
    position = jnp.cumsum(tile_seen, dtype=jnp.int32) - 1
    slot_ids = jnp.arange(slot_count, dtype=jnp.int32)
    hits = (position[None, :] == slot_ids[:, None]) & (tile_seen[None, :] == 1)
    return (hits.astype(jnp.bfloat16), position)

def attend(query, keys, values, key_valid):
    query_count = query.shape[0]
    key_count = keys.shape[0]
    query_heads = query.astype(jnp.float32).reshape(query_count, HEADS, HEAD_DIM)
    key_heads = keys.astype(jnp.float32).reshape(key_count, HEADS, HEAD_DIM)
    value_heads = values.astype(jnp.float32).reshape(key_count, HEADS, HEAD_DIM)
    scores = jnp.einsum('qhd,khd->hqk', query_heads, key_heads) * (1.0 / math.sqrt(HEAD_DIM))
    scores = jnp.where(key_valid[None, None, :], scores, -1e+30)
    probs = jax.nn.softmax(scores, axis=-1).astype(jnp.bfloat16)
    attended = jnp.einsum('hqk,khd->qhd', probs.astype(jnp.float32), value_heads)
    return attended.reshape(query_count, HEADS * HEAD_DIM).astype(jnp.bfloat16)

def decode(embedded, selector, position, tile_seen, tile_targets, mask_token, tile_pos, w_up, w_down, w_head, grad_scale):
    seen_rows = (tile_seen == 1)[:, None]
    spread = jnp.take(embedded, jnp.clip(position, 0, embedded.shape[0] - 1), axis=0)
    stream = jnp.where(seen_rows, spread, mask_token.astype(jnp.float32)[None, :]) + tile_pos.astype(jnp.float32)
    unit = layer_norm(stream).astype(jnp.bfloat16)
    hidden_in = jnp.dot(unit, w_up, preferred_element_type=jnp.float32)
    active = gelu_exact(hidden_in).astype(jnp.bfloat16)
    stream_out = stream + jnp.dot(active, w_down, preferred_element_type=jnp.float32)
    predicted = jnp.dot(stream_out.astype(jnp.bfloat16), w_head, preferred_element_type=jnp.float32)
    pred_grad = ((predicted - tile_targets.astype(jnp.float32)) * grad_scale).astype(jnp.bfloat16)
    out_grad = jnp.dot(pred_grad, w_head.T, preferred_element_type=jnp.float32)
    out_grad_low = out_grad.astype(jnp.bfloat16)
    grad_down = jnp.dot(active.T, out_grad_low, preferred_element_type=jnp.float32)
    active_grad = jnp.dot(out_grad_low, w_down.T, preferred_element_type=jnp.float32)
    hidden_grad = (active_grad * gelu_slope(hidden_in)).astype(jnp.bfloat16)
    grad_up = jnp.dot(unit.T, hidden_grad, preferred_element_type=jnp.float32)
    unit_grad = jnp.dot(hidden_grad, w_up.T, preferred_element_type=jnp.float32)
    stream_grad = out_grad + norm_backward(stream, unit_grad)
    row_grad = jnp.where(seen_rows, stream_grad, 0.0).astype(jnp.bfloat16)
    slot_grad = jnp.dot(selector, row_grad, preferred_element_type=jnp.float32).astype(jnp.bfloat16)
    return (slot_grad, grad_up, grad_down)

def reference(tokens, targets, visible, w_qkv, w_out, w_embed, mask_token, dec_pos, w_up, w_down, w_head):
    grad_scale = 8.0 / math.sqrt(MASKED)
    pos_tiles = dec_pos.reshape(N_BLK, TILE, DEC_WIDTH)

    def one_scene(carry, pieces):
        scene_rows, scene_targets, scene_seen = pieces
        rows_tiled = scene_rows.reshape(N_BLK, TILE, D)
        targets_tiled = scene_targets.reshape(N_BLK, TILE, PATCH_PIXELS)
        seen_tiled = scene_seen.reshape(N_BLK, TILE)
        selector, position = jax.vmap(lambda tile_seen: slot_table(tile_seen, TILE_CAP))(seen_tiled)
        packed = jnp.einsum('tcp,tpd->tcd', selector.astype(jnp.float32), rows_tiled.astype(jnp.float32)).astype(jnp.bfloat16)
        packed_flat = packed.reshape(N_BLK * TILE_CAP, D)
        normed = layer_norm(packed_flat.astype(jnp.float32)).astype(jnp.bfloat16)
        projected = jnp.dot(normed, w_qkv, preferred_element_type=jnp.float32).astype(jnp.bfloat16)
        counts = lax.optimization_barrier(jnp.sum(seen_tiled, axis=1, dtype=jnp.int32))
        key_valid = (jnp.arange(TILE_CAP, dtype=jnp.int32)[None, :] < counts[:, None]).reshape(N_BLK * TILE_CAP)
        attended = attend(projected[:, :INNER], projected[:, INNER:2 * INNER], projected[:, 2 * INNER:], key_valid)
        encoded = (packed_flat.astype(jnp.float32) + jnp.dot(attended, w_out, preferred_element_type=jnp.float32)).astype(jnp.bfloat16)
        embedded = jnp.dot(encoded, w_embed, preferred_element_type=jnp.float32).reshape(N_BLK, TILE_CAP, DEC_WIDTH)
        slot_grad, grad_up, grad_down = jax.vmap(decode, in_axes=(0, 0, 0, 0, 0, None, 0, None, None, None, None))(embedded, selector, position, seen_tiled, targets_tiled, mask_token, pos_tiles, w_up, w_down, w_head, grad_scale)
        encoded_grad = jnp.dot(slot_grad.reshape(N_BLK * TILE_CAP, DEC_WIDTH), w_embed.T, preferred_element_type=jnp.float32).astype(jnp.bfloat16)
        grad_out = jnp.dot(attended.T, encoded_grad, preferred_element_type=jnp.float32)
        carry = (carry[0] + grad_out, carry[1] + lax.optimization_barrier(jnp.sum(grad_up, axis=0)), carry[2] + lax.optimization_barrier(jnp.sum(grad_down, axis=0)))
        return (carry, None)
    start = (jnp.zeros((INNER, D), jnp.float32), jnp.zeros((DEC_WIDTH, FF), jnp.float32), jnp.zeros((FF, DEC_WIDTH), jnp.float32))
    totals, _ = lax.scan(one_scene, start, (tokens, targets, visible))
    return (totals[0], totals[1], totals[2])
```

```python
import math

import jax
import jax.numpy as jnp
from jax import lax
from jax.experimental import pallas as pl
from jax.experimental.pallas import tpu as pltpu
from jax.sharding import PartitionSpec as P

MESH = pl.DeviceIdType.MESH
F32 = jnp.float32
BF16 = jnp.bfloat16

HEADS = 8
HEAD_DIM = 80
VIS_TILE = 96
TILE = 384
CAP = 168
ROWS = 176
D = 1280
DEC = 512
FF = 1024
PIX = 1176
INNER = 640
HALF = 192
SLOTS = 96
SEG_STEP = 80
EPS = 1e-05
OUT_MASK = -1e30


def dot(a, b):
    return lax.dot_general(a, b, (((1,), (0,)), ((), ())), preferred_element_type=F32)


def dot_nt(a, b):
    return lax.dot_general(a, b, (((1,), (1,)), ((), ())), preferred_element_type=F32)


def dot_tn(a, b):
    return lax.dot_general(a, b, (((0,), (0,)), ((), ())), preferred_element_type=F32)


def normalize(rows):
    center = rows - jnp.mean(rows, axis=-1, keepdims=True)
    inverse = lax.rsqrt(jnp.mean(center * center, axis=-1, keepdims=True) + EPS)
    return center * inverse, inverse


def iota(shape, axis):
    return lax.broadcasted_iota(jnp.int32, shape, axis)


names = []


def ident(name):
    if name not in names:
        names.append(name)
    return names.index(name)


N_REMOTE = 96
N_LOCAL = 32


def kernel(
    tokens_h, targets_h, vis_ref, wqkv_h, wout_h, wembed_h, mtok_ref, dpos_h, wup_h, wdown_h, whead_h,
    go_ref, gu_ref, gd_ref,
    tokens, targets, wqkv, wout, wembed, dpos, wup, wdown, whead, wperm,
    selector, seen_col, packed, heads, other, kv_own, kv_r, kv_l, kv_d, keys, vals, qx, acc, top,
    att_out, att_in, att, att_sib, pos_slot, tgt_slot, mask_slot,
    unit_m, act_m, og_m, hg_m, unit_ms, act_ms, og_ms, hg_ms, gd_acc, gu_acc,
    unit_v, act_v, og_v, hg_v, sg_v, unit_vs, act_vs, og_vs, hg_vs, sg_vs,
    rs_gd, rs_gu, rs_p, rs_q, rs_x2, rs_y2,
    in_gd, in_gu, in_p, in_q, in_x2, in_y2,
    turned, zs, zr,
    send_sem, recv_sem, load_sem,
):
    dp = lax.axis_index("dp")
    seg = lax.axis_index("segment")
    blk = lax.axis_index("blk")
    x, core = dp // 2, dp % 2
    y, z = seg * 2 + blk // 8, blk % 8
    y_lo = blk // 8

    def device(px, pc, py, pz):
        return (px * 2 + pc, py // 2, (py % 2) * 8 + pz)

    def at_x(step):
        return device((x + step + 4) % 4, core, y, z)

    def at_y(step):
        return device(x, core, (y + step + 4) % 4, z)

    def at_z(step):
        return device(x, core, y, (z + step + 8) % 8)

    sibling = device(x, 1 - core, y, z)

    loads = {}

    def load(name, src, dst):
        copy = pltpu.make_async_copy(src, dst, load_sem.at[len(loads)])
        copy.start()
        loads[name] = copy

    load("tokens", tokens_h, tokens)
    load("wqkv", wqkv_h, wqkv)
    load("dpos", dpos_h, dpos)
    load("targets", targets_h, targets)
    load("wup", wup_h, wup)
    load("wdown", wdown_h, wdown)
    load("whead", whead_h, whead)
    load("wout", wout_h, wout)
    load("wembed", wembed_h, wembed)
    for px in range(4):
        for ps in range(2):
            first = pl.multiple_of((px * 4 + core * 2 + ps) * 80, 16)
            load(
                "wp%d%d" % (px, ps),
                wembed_h.at[pl.ds(first, 48)],
                wperm.at[pl.ds(px * 96 + ps * 48, 48)],
            )
            load(
                "wq%d%d" % (px, ps),
                wembed_h.at[pl.ds(pl.multiple_of(first + 48, 16), 32)],
                wperm.at[pl.ds(384 + ps * 128 + px * 32, 32)],
            )

    barrier = pltpu.get_barrier_semaphore()
    peers = [sibling, at_x(1), at_x(-1), at_y(1), at_y(-1), at_y(2)]
    peers += [at_z(step) for step in range(1, 8)]
    for peer in peers:
        pl.semaphore_signal(barrier, inc=1, device_id=peer, device_id_type=MESH)

    started = []

    def send(name, src, dst, target):
        i = ident(name)
        copy = pltpu.make_async_remote_copy(
            src_ref=src,
            dst_ref=dst,
            send_sem=send_sem.at[i],
            recv_sem=recv_sem.at[i],
            device_id=target,
            device_id_type=MESH,
        )
        copy.start()
        started.append(copy)
        return copy

    vis = vis_ref[...].astype(F32)
    tri = (iota((TILE, TILE), 0) <= iota((TILE, TILE), 1)).astype(F32).astype(BF16)
    vis8 = jnp.broadcast_to(vis, (8, TILE))
    position = dot(vis8.astype(BF16), tri)[0:1, :] - 1.0
    count = jnp.sum(vis, axis=1, keepdims=True)
    slot_ids = iota((ROWS, TILE), 0).astype(F32)
    chosen = jnp.where((position == slot_ids) & (vis > 0.5), 1.0, 0.0).astype(BF16)
    selector[...] = chosen
    loads["tokens"].wait()
    rows = dot(chosen, tokens[...])
    packed[...] = rows.astype(BF16)
    normed = normalize(rows)[0].astype(BF16)
    seen_col[...] = dot_tn(chosen, jnp.ones((ROWS, 128), BF16))
    loads["wqkv"].wait()
    projected = dot(normed, wqkv[...])
    slot_row = iota((ROWS, 256), 0)
    for h in range(HEADS):
        parts = [projected[:, o + h * 80 : o + h * 80 + 80] for o in (640, 1280, 0)]
        block = jnp.concatenate(parts + [jnp.zeros((ROWS, 16), F32)], axis=1)
        block = jnp.where(slot_row >= CAP, count, block)
        heads[h] = block.astype(BF16)

    pl.semaphore_wait(barrier, len(peers))
    up_head = ((y + 1) % 4) * 2
    down_head = ((y + 3) % 4) * 2 + 1
    from_down = send("qkv+", heads.at[up_head], other.at[0], at_y(1))
    from_up = send("qkv-", heads.at[down_head], other.at[1], at_y(-1))

    lane = iota((ROWS, 128), 1)
    slot128 = iota((ROWS, 128), 0).astype(F32)

    def make_query(block, j, first):
        window = pltpu.roll(block[:, 128:256].astype(F32), 96, 1)
        query = jnp.where(lane < 80, window, jnp.where(lane == 80, 1.0, 0.0))
        qx[j, first : first + ROWS, :] = query.astype(BF16)

    def pick_kv(block):
        return block[:, 0:160].astype(F32)

    own = [heads[y * 2], heads[y * 2 + 1]]
    from_down.wait_recv()
    from_up.wait_recv()
    others = [other[0], other[1]]
    kv = [pick_kv(b) for b in own + others]
    kv_own[...] = jnp.concatenate(kv, axis=1).astype(BF16)

    cut = ((0, 96), (96, 80))

    def ring_send(name, src, dst, part, target):
        first, length = cut[part]
        return send(
            name + str(part), src.at[pl.ds(first, length)], dst.at[pl.ds(first, length)], target
        )

    ring = {}
    for part in range(2):
        ring["r0", part] = ring_send("r0", kv_own, kv_r.at[0], part, at_z(1))
        ring["l0", part] = ring_send("l0", kv_own, kv_l.at[0], part, at_z(-1))

    def ring_step(step):
        for part in range(2):
            ring["r%d" % (step - 1), part].wait_recv()
            if step < 3:
                ring["r%d" % step, part] = ring_send(
                    "r%d" % step, kv_r.at[step - 1], kv_r.at[step], part, at_z(1)
                )
            elif part == 0:
                ring["d", 0] = ring_send("d", kv_r.at[2], kv_d, 0, at_z(1))
            ring["l%d" % (step - 1), part].wait_recv()
            if step < 3:
                ring["l%d" % step, part] = ring_send(
                    "l%d" % step, kv_l.at[step - 1], kv_l.at[step], part, at_z(-1)
                )
            elif part == 1:
                ring["d", 1] = ring_send("d", kv_l.at[2], kv_d, 1, at_z(-1))

    def unpack(block, first):
        for i in range(2):
            for j in range(2):
                base = 320 * i + 160 * j
                low = base // 128 * 128
                window = block[:, low : low + 256].astype(F32)
                off = base % 128
                key = window if off == 0 else pltpu.roll(window, 256 - off, 1)
                key = key[:, 0:128]
                value = pltpu.roll(window, 256 - off - 80, 1)[:, 0:128]
                counts = key[CAP : CAP + 1, :]
                outside = jnp.where((lane == 80) & (slot128 >= counts), OUT_MASK, 0.0)
                at = first + i * ROWS
                keys[j, at : at + ROWS, :] = jnp.where(lane < 80, key, outside).astype(BF16)
                vals[j, at : at + ROWS, :] = jnp.where(lane == 80, 1.0, value).astype(BF16)

    scale = math.log2(math.e) / math.sqrt(HEAD_DIM)

    def attend(first, length, begin=False):
        for j in range(2):
            scores = dot_nt(qx[j], keys[j, first : first + length, :])
            best = jnp.max(scores, axis=1, keepdims=True)
            if not begin:
                before = top[j]
                best = jnp.maximum(before[:, 0:1], best)
            probs = jnp.exp2((scores - best) * scale).astype(BF16)
            term = dot(probs, vals[j, first : first + length, :])
            if not begin:
                term = term + acc[j] * jnp.exp2((before - best) * scale)
            acc[j] = term
            top[j] = jnp.broadcast_to(best, (2 * ROWS, 128))

    grad_scale = 8.0 / math.sqrt(8 * 16 * (TILE - VIS_TILE))
    root_half = 1.0 / math.sqrt(2.0)
    order = iota((DEC, DEC), 1)
    source = (order // 32 % 4) * 128 + (order // 256) * 64 + (order // 128 % 2) * 32 + order % 32
    shuffle = (iota((DEC, DEC), 0) == source).astype(F32).astype(BF16)

    def decode_forward(stream, goal, keep, unit, act):
        normal, inverse = normalize(stream)
        low = normal.astype(BF16)
        unit[...] = low
        hidden = dot(low, wup[...])
        cumulative = 0.5 * (1.0 + lax.erf(hidden * root_half))
        active = (hidden * cumulative).astype(BF16)
        act[...] = active
        slope = cumulative + hidden * jnp.exp(-0.5 * hidden * hidden) * (
            1.0 / math.sqrt(2.0 * math.pi)
        )
        stream_out = stream + dot(active, wdown[...])
        predicted = dot(stream_out.astype(BF16), whead[...])
        pred_grad = ((predicted - goal) * (keep * grad_scale)).astype(BF16)
        out_grad = dot_nt(pred_grad, whead[...])
        return normal, inverse, slope, out_grad

    def decode_hidden(out_low, slope, hg):
        hidden_grad = (dot_nt(out_low, wdown[...]) * slope).astype(BF16)
        for c in range(2):
            for px in range(4):
                at = px * 256 + c * 128
                hg[c, :, px * 128 : px * 128 + 128] = hidden_grad[:, at : at + 128]
        return hidden_grad

    def split_out(out_low, og):
        mixed = dot(out_low, shuffle).astype(BF16)
        og[0] = mixed[:, 0:256]
        og[1] = mixed[:, 256:512]

    for j in range(2):
        make_query(own[j], j, 0)
        make_query(others[j], j, ROWS)
    unpack(kv_own, 0)
    attend(0, 2 * ROWS, begin=True)
    for name in ("dpos", "targets", "wup", "wdown", "whead"):
        loads[name].wait()
    ring_step(1)

    part_rows = pl.ds(pl.multiple_of(seg * HALF, 16), HALF)
    stream_m = mtok_ref[...].astype(F32) + dpos[part_rows, :].astype(F32)
    goal_m = targets[part_rows, :].astype(F32)
    keep_m = 1.0 - seen_col[part_rows, :][:, 0:1]
    normal, inverse, slope, out_grad = decode_forward(stream_m, goal_m, keep_m, unit_m, act_m)
    out_low = out_grad.astype(BF16)
    split_out(out_low, og_m)
    decode_hidden(out_low, slope, hg_m)
    masked = [
        send("unit_m", unit_m, unit_ms, sibling),
        send("act_m", act_m, act_ms, sibling),
        send("og_m", og_m.at[1 - core], og_ms, sibling),
        send("hg_m", hg_m.at[1 - core], hg_ms, sibling),
    ]
    unpack(kv_r.at[0], 2 * ROWS)
    unpack(kv_l.at[0], 4 * ROWS)
    attend(2 * ROWS, 4 * ROWS)
    ring_step(2)

    slot_first = pl.multiple_of(seg * SEG_STEP, 16)
    slot_rows = pl.ds(slot_first, SLOTS)
    chosen_part = selector[slot_rows, :]
    pos_slot[...] = dot(chosen_part, dpos[...])
    tgt_slot[...] = dot(chosen_part, targets[...])
    number = iota((SLOTS, 128), 0) + seg * SEG_STEP
    kept = (number.astype(F32) < count) & (number >= seg * SLOTS)
    mask_slot[...] = jnp.where(kept, 1.0, 0.0)

    for copy in masked:
        copy.wait_recv()
    gd_acc[...] = dot_tn(og_m[core], act_m[...]) + dot_tn(og_ms[...], act_ms[...])
    gu_acc[...] = dot_tn(unit_m[...], hg_m[core]) + dot_tn(unit_ms[...], hg_ms[...])
    unpack(kv_r.at[1], 6 * ROWS)
    unpack(kv_l.at[1], 8 * ROWS)
    attend(6 * ROWS, 4 * ROWS)
    ring_step(3)
    unpack(kv_r.at[2], 10 * ROWS)
    unpack(kv_l.at[2], 12 * ROWS)
    attend(10 * ROWS, 4 * ROWS)
    for name in loads:
        if name not in ("tokens", "wqkv", "dpos", "targets", "wup", "wdown", "whead"):
            loads[name].wait()
    ring["d", 0].wait_recv()
    ring["d", 1].wait_recv()
    unpack(kv_d, 14 * ROWS)
    attend(14 * ROWS, 2 * ROWS)

    done = []
    for j in range(2):
        total = acc[j]
        done.append((total * (1.0 / total[:, 80:81]))[:, 0:80])
    both = jnp.concatenate(done + [jnp.zeros((2 * ROWS, 96), F32)], axis=1).astype(BF16)
    att_out[0] = both[0:ROWS]
    att_out[1] = both[ROWS : 2 * ROWS]
    back = []
    for step, i in ((2, 0), (1, 1), (-1, 1)):
        goal_seg = ((y + step + 4) % 4) // 2
        span = pl.ds(pl.multiple_of(goal_seg * SEG_STEP, 16), SLOTS)
        back.append(send("att%d" % (step + 4), att_out.at[i, span], att_in.at[y], at_y(step)))
    att_in[y] = att_out[0, slot_rows, :]
    for copy in back:
        copy.wait_recv()
    attended = jnp.concatenate([att_in[i][:, 0:160].astype(F32) for i in range(4)], axis=1)
    attended = attended.astype(BF16)
    att[...] = attended
    swap_att = send("att_s", att, att_sib, sibling)

    encoded = packed[slot_rows, :].astype(F32) + dot(attended, wout[...])
    embedded = dot(encoded.astype(BF16), wembed[...])
    stream_v = embedded + pos_slot[...]
    normal, inverse, slope, out_grad = decode_forward(
        stream_v, tgt_slot[...], mask_slot[:, 0:1], unit_v, act_v
    )
    swap_unit = send("unit_v", unit_v, unit_vs, sibling)
    swap_act = send("act_v", act_v, act_vs, sibling)
    out_low = out_grad.astype(BF16)
    split_out(out_low, og_v)
    swap_og = send("og_v", og_v.at[1 - core], og_vs, sibling)
    hidden_grad = decode_hidden(out_low, slope, hg_v)
    swap_hg = send("hg_v", hg_v.at[1 - core], hg_vs, sibling)
    unit_grad = dot_nt(hidden_grad, wup[...])
    cross = jnp.mean(unit_grad * normal, axis=-1, keepdims=True)
    middle = jnp.mean(unit_grad, axis=-1, keepdims=True)
    stream_grad = out_grad + inverse * (unit_grad - middle - normal * cross)
    sg_v[...] = stream_grad.astype(BF16)
    swap_sg = send("sg_v", sg_v, sg_vs, sibling)

    def ring_sum(name, chunks, landing, h0, h1, place, at):
        right, left, far = (place + 1) % 4, (place + 3) % 4, (place + 2) % 4
        s0, s1 = pl.ds(0, h0), pl.ds(h0, h1)
        rel0 = send(name + "rel0", chunks.at[far, s0], landing.at[0, s0], at(1))
        rel1 = send(name + "rel1", chunks.at[far, s1], landing.at[0, s1], at(-1))
        dir1 = send(name + "dir1", chunks.at[right, s1], landing.at[1, s1], at(1))
        dir0 = send(name + "dir0", chunks.at[left, s0], landing.at[1, s0], at(-1))
        state = {}

        def relay():
            rel0.wait_recv()
            landing[3, s0, :] = (
                landing[0, s0, :].astype(F32) + chunks[right, s0, :].astype(F32)
            ).astype(BF16)
            state["c0"] = send(name + "c0", landing.at[3, s0], landing.at[2, s0], at(1))
            rel1.wait_recv()
            landing[3, s1, :] = (
                landing[0, s1, :].astype(F32) + chunks[left, s1, :].astype(F32)
            ).astype(BF16)
            state["c1"] = send(name + "c1", landing.at[3, s1], landing.at[2, s1], at(-1))

        def finish():
            dir0.wait_recv()
            dir1.wait_recv()
            state["c0"].wait_recv()
            state["c1"].wait_recv()
            return (
                chunks[place].astype(F32) + landing[1].astype(F32) + landing[2].astype(F32)
            )

        return relay, finish

    swap_act.wait_recv()
    swap_og.wait_recv()
    gd_t = gd_acc[...] + dot_tn(og_v[core], act_v[...]) + dot_tn(og_vs[...], act_vs[...])
    gd_t = gd_t.astype(BF16)
    for py in range(4):
        for px in range(4):
            for k in range(4):
                r = (py // 2) * 128 + px * 32
                c = (py % 2) * 512 + k * 128
                at = px * 128 + k * 32
                rs_gd[py, at : at + 32, :] = gd_t[r : r + 32, c : c + 128]
    relay_gd, finish_gd = ring_sum("gd", rs_gd, in_gd, 256, 256, y, at_y)

    swap_unit.wait_recv()
    swap_hg.wait_recv()
    gu_t = gu_acc[...] + dot_tn(unit_v[...], hg_v[core]) + dot_tn(unit_vs[...], hg_vs[...])
    gu_t = gu_t.astype(BF16)
    for px in range(4):
        rs_gu[px] = gu_t[:, px * 128 : px * 128 + 128]
    relay_gu, finish_gu = ring_sum("gu", rs_gu, in_gu, 256, 256, x, at_x)

    swap_att.wait_recv()
    swap_sg.wait_recv()
    eg = dot_nt(sg_v[...], wperm[...]).astype(BF16)
    eg_s = dot_nt(sg_vs[...], wperm[...]).astype(BF16)
    go_t = (dot_tn(eg, att[...]) + dot_tn(eg_s, att_sib[...])).astype(BF16)
    for px in range(4):
        for k in range(5):
            rs_p[px, 96 * k : 96 * k + 96, :] = go_t[px * 96 : px * 96 + 96, k * 128 : k * 128 + 128]
    relay_p, finish_p = ring_sum("p", rs_p, in_p, 240, 240, x, at_x)
    for py in range(4):
        for px in range(4):
            for k in range(3):
                r = 384 + (py // 2) * 128 + px * 32
                c = ((py % 2) * 2 + k) * 128
                at = px * 96 + k * 32
                rs_q[py, at : at + 32, :] = go_t[r : r + 32, c : c + 128]
    relay_q, finish_q = ring_sum("q", rs_q, in_q, 192, 192, y, at_y)

    relay_gd()
    relay_gu()
    relay_p()
    relay_q()

    gd_1 = finish_gd()
    q_1 = finish_q()
    for px in range(4):
        rs_y2[px, 0:128, :] = gd_1[px * 128 : px * 128 + 128].astype(BF16)
        rs_y2[px, 128:224, :] = q_1[px * 96 : px * 96 + 96].astype(BF16)
    relay_y2, finish_y2 = ring_sum("y2", rs_y2, in_y2, 112, 112, x, at_x)
    gu_1 = finish_gu()
    p_1 = finish_p()
    lane128 = iota((128, 128), 1)
    for py in range(4):
        first = gu_1[(py % 2) * 256 : (py % 2) * 256 + 128]
        second = gu_1[(py % 2) * 256 + 128 : (py % 2) * 256 + 256]
        if py // 2 == 0:
            pair = jnp.where(lane128 < 64, first, pltpu.roll(second, 64, 1))
        else:
            pair = jnp.where(lane128 < 64, pltpu.roll(first, 64, 1), second)
        rs_x2[py, 0:128, :] = pair.astype(BF16)
        for k in range(3):
            r = 96 * ((py % 2) * 2 + k) + (py // 2) * 48
            rs_x2[py, 128 + 48 * k : 176 + 48 * k, :] = p_1[r : r + 48].astype(BF16)
    relay_x2, finish_x2 = ring_sum("x2", rs_x2, in_x2, 144, 128, y, at_y)
    relay_y2()
    relay_x2()
    y_2 = finish_y2()
    x_2 = finish_x2()

    p_rows = jnp.concatenate([x_2[128 + 48 * k : 176 + 48 * k] for k in range(3)], axis=1)
    q_rows = jnp.concatenate([y_2[128 + 32 * k : 160 + 32 * k] for k in range(3)], axis=1)
    go_rows = jnp.concatenate([p_rows, q_rows, jnp.zeros((48, 384), F32)], axis=0)
    turned[0:384, :] = go_rows.T
    turned[384:400, :] = jnp.zeros((16, 128), F32)
    lane32 = iota((32, 128), 1)
    for pz in range(8):
        up = x_2[(pz % 4) * 32 : (pz % 4) * 32 + 32]
        if pz // 4 == 1:
            up = pltpu.roll(up, 64, 1)
        down = y_2[(pz // 2) * 32 : (pz // 2) * 32 + 32]
        if pz % 2 == 0:
            down = pltpu.roll(down, 64, 1)
        zs[pz, 0:32, :] = jnp.where(lane32 < 64, up, down).astype(BF16)
        at = pl.multiple_of(y_lo * 64 + pz * 40, 8)
        zs[pz, 32:80, :] = turned[pl.ds(at, 48), :].astype(BF16)
    last = []
    for step in range(1, 8):
        last.append(send("z%d" % step, zs.at[(z + step) % 8], zr.at[step - 1], at_z(step)))
    result = zs[z].astype(F32)
    for step in range(1, 8):
        last[step - 1].wait_recv()
        result = result + zr[step - 1].astype(F32)
    go_ref[...] = result[32:72, 0:80]
    gu_ref[...] = result[0:32, 0:64]
    gd_ref[...] = result[0:32, :].T[64:128, :]

    for copy in started:
        copy.wait_send()


def on_device(
    tokens, targets, visible, w_qkv, w_out, w_embed, mask_token, dec_pos, w_up, w_down, w_head
):
    names.clear()
    anywhere = pl.BlockSpec(memory_space=pl.ANY)
    vmem = pl.BlockSpec(memory_space=pltpu.VMEM)

    def low(*shape):
        return pltpu.VMEM(shape, BF16)

    def wide(*shape):
        return pltpu.VMEM(shape, F32)

    scratch = [
        low(TILE, D), low(TILE, PIX), low(D, 3 * INNER), low(INNER, D), low(D, DEC),
        low(TILE, DEC), low(DEC, FF), low(FF, DEC), low(DEC, PIX), low(INNER, DEC),
        low(ROWS, TILE), wide(TILE, 128), low(ROWS, D), low(HEADS, ROWS, 256), low(2, ROWS, 256),
        low(ROWS, INNER), low(3, ROWS, INNER), low(3, ROWS, INNER), low(ROWS, INNER),
        low(2, 16 * ROWS, 128), low(2, 16 * ROWS, 128), low(2, 2 * ROWS, 128),
        wide(2, 2 * ROWS, 128), wide(2, 2 * ROWS, 128),
        low(2, ROWS, 256), low(4, SLOTS, 256), low(SLOTS, INNER), low(SLOTS, INNER),
        wide(SLOTS, DEC), wide(SLOTS, PIX), wide(SLOTS, 128),
        low(HALF, DEC), low(HALF, FF), low(2, HALF, 256), low(2, HALF, DEC),
        low(HALF, DEC), low(HALF, FF), low(HALF, 256), low(HALF, DEC),
        wide(256, FF), wide(DEC, DEC),
        low(SLOTS, DEC), low(SLOTS, FF), low(2, SLOTS, 256), low(2, SLOTS, DEC), low(SLOTS, DEC),
        low(SLOTS, DEC), low(SLOTS, FF), low(SLOTS, 256), low(SLOTS, DEC), low(SLOTS, DEC),
        low(4, 512, 128), low(4, 512, 128), low(4, 480, 128), low(4, 384, 128),
        low(4, 272, 128), low(4, 224, 128),
        low(4, 512, 128), low(4, 512, 128), low(4, 480, 128), low(4, 384, 128),
        low(4, 272, 128), low(4, 224, 128),
        wide(400, 128), low(8, 80, 128), low(7, 80, 128),
        pltpu.SemaphoreType.DMA((N_REMOTE,)),
        pltpu.SemaphoreType.DMA((N_REMOTE,)),
        pltpu.SemaphoreType.DMA((N_LOCAL,)),
    ]
    return pl.pallas_call(
        kernel,
        out_shape=(
            jax.ShapeDtypeStruct((40, 80), F32),
            jax.ShapeDtypeStruct((32, 64), F32),
            jax.ShapeDtypeStruct((64, 32), F32),
        ),
        in_specs=[
            anywhere, anywhere, vmem, anywhere, anywhere, anywhere, vmem, anywhere, anywhere,
            anywhere, anywhere,
        ],
        out_specs=(vmem, vmem, vmem),
        scratch_shapes=scratch,
        compiler_params=pltpu.CompilerParams(
            collective_id=0, has_side_effects=True, vmem_limit_bytes=56 * 1024 * 1024
        ),
    )(
        tokens[0], targets[0], visible, w_qkv, w_out, w_embed, mask_token[None, :], dec_pos, w_up,
        w_down, w_head,
    )


def solution(mesh):
    in_specs = (
        P("dp", "blk", None),
        P("dp", "blk", None),
        P("dp", "blk"),
        P(),
        P(),
        P(),
        P(),
        P("blk", None),
        P(),
        P(),
        P(),
    )
    out_specs = (
        P("blk", ("dp", "segment")),
        P("blk", ("dp", "segment")),
        P("blk", ("dp", "segment")),
    )
    return jax.shard_map(
        on_device, mesh=mesh, in_specs=in_specs, out_specs=out_specs, check_vma=False
    )
```

```python
import math

import jax
import jax.numpy as jnp
from jax import lax
from jax.experimental import pallas as pl
from jax.experimental.pallas import tpu as pltpu
from jax.sharding import PartitionSpec as P

MESH = pl.DeviceIdType.MESH
F32 = jnp.float32
BF16 = jnp.bfloat16

HEADS = 8
HEAD_DIM = 80
VIS_TILE = 96
TILE = 384
CAP = 168
ROWS = 176
D = 1280
DEC = 512
FF = 1024
PIX = 1176
INNER = 640
HALF = 192
SLOTS = 96
SEG_STEP = 80
PART = 448
EPS = 1e-05
OUT_MASK = -1e30


def dot(a, b):
    return lax.dot_general(a, b, (((1,), (0,)), ((), ())), preferred_element_type=F32)


def dot_nt(a, b):
    return lax.dot_general(a, b, (((1,), (1,)), ((), ())), preferred_element_type=F32)


def dot_tn(a, b):
    return lax.dot_general(a, b, (((0,), (0,)), ((), ())), preferred_element_type=F32)


def normalize(rows):
    center = rows - jnp.mean(rows, axis=-1, keepdims=True)
    inverse = lax.rsqrt(jnp.mean(center * center, axis=-1, keepdims=True) + EPS)
    return center * inverse, inverse


def iota(shape, axis):
    return lax.broadcasted_iota(jnp.int32, shape, axis)


names = []


def ident(name):
    if name not in names:
        names.append(name)
    return names.index(name)


N_REMOTE = 128
N_LOCAL = 32


def kernel(
    tokens_h, targets_h, vis_ref, wqkv_h, wout_h, wembed_h, mtok_ref, dpos_h, wup_h, wdown_h, whead_h,
    sums_ref,
    tokens, targets, wq, wk, wv, wout, wembed, dpos, wup, wdown, whead,
    selector, seen_col, packed, heads, other, kv_own, kv_r, kv_l, keys, vals, qx, acc, top,
    att_out, att_in, att, att_sib, pos_slot, tgt_slot, mask_slot,
    unit_m, act_m, og_m, hg_m, unit_ms, act_ms, og_ms, hg_ms, gd_acc, gu_acc,
    unit_v, act_v, og_v, hg_v, sg_v, unit_vs, act_vs, og_vs, hg_vs, sg_vs,
    rs_gd, rs_gu, rs_g, rs_h, rs_x2, rs_y2,
    in_gd, in_gu, in_g, in_h, in_x2, in_y2,
    zs, zr, zg, zgr, ag, gr,
    send_sem, recv_sem, load_sem,
):
    dp = lax.axis_index("dp")
    seg = lax.axis_index("segment")
    blk = lax.axis_index("blk")
    x, core = dp // 2, dp % 2
    y, z = seg * 2 + blk // 8, blk % 8
    y_lo = blk // 8

    def device(px, pc, py, pz):
        return (px * 2 + pc, py // 2, (py % 2) * 8 + pz)

    def at_x(step):
        return device((x + step + 4) % 4, core, y, z)

    def at_y(step):
        return device(x, core, (y + step + 4) % 4, z)

    def at_z(step):
        return device(x, core, y, (z + step + 8) % 8)

    sibling = device(x, 1 - core, y, z)

    loads = {}

    def load(name, src, dst):
        copy = pltpu.make_async_copy(src, dst, load_sem.at[len(loads)])
        copy.start()
        loads[name] = copy

    load("tokens", tokens_h, tokens)
    for name, dst, first in (("wk", wk, 640), ("wv", wv, 1280), ("wq", wq, 0)):
        for part in range(2):
            span = pl.ds(part * 640, 640)
            load(name + str(part), wqkv_h.at[span, pl.ds(first, 640)], dst.at[span])

    barrier = pltpu.get_barrier_semaphore()
    peers = [at_z(step) for step in range(1, 8)]
    for px in range(4):
        for pc in range(2):
            for py in range(4):
                if px or pc or py:
                    peers.append(device((x + px) % 4, (core + pc) % 2, (y + py) % 4, z))
    for peer in peers:
        pl.semaphore_signal(barrier, inc=1, device_id=peer, device_id_type=MESH)

    started = []

    def describe(name, src, dst, target, landed=None):
        return pltpu.make_async_remote_copy(
            src_ref=src,
            dst_ref=dst,
            send_sem=send_sem.at[ident(name)],
            recv_sem=recv_sem.at[ident(landed or name)],
            device_id=target,
            device_id_type=MESH,
        )

    def send(name, src, dst, target):
        copy = describe(name, src, dst, target)
        copy.start()
        started.append(copy)
        return copy

    vis = vis_ref[...].astype(F32)
    tri = (iota((TILE, TILE), 0) <= iota((TILE, TILE), 1)).astype(F32).astype(BF16)
    vis8 = jnp.broadcast_to(vis, (8, TILE))
    position = dot(vis8.astype(BF16), tri)[0:1, :] - 1.0
    count = jnp.sum(vis, axis=1, keepdims=True)
    slot_ids = iota((ROWS, TILE), 0).astype(F32)
    chosen = jnp.where((position == slot_ids) & (vis > 0.5), 1.0, 0.0).astype(BF16)
    selector[...] = chosen
    loads["tokens"].wait()
    rows = dot(chosen, tokens[...])
    packed[...] = rows.astype(BF16)
    normed = normalize(rows)[0].astype(BF16)
    seen_col[...] = dot_tn(chosen, jnp.ones((ROWS, 128), BF16))
    projected = []
    for name, weight in (("wk", wk), ("wv", wv), ("wq", wq)):
        loads[name + "0"].wait()
        loads[name + "1"].wait()
        projected.append(dot(normed, weight[...]))
    load("dpos", dpos_h, dpos)
    load("targets", targets_h, targets)
    load("wup", wup_h, wup)
    load("wdown", wdown_h, wdown)
    load("whead", whead_h, whead)
    load("wout", wout_h, wout)
    load("wembed", wembed_h, wembed)
    slot_row = iota((ROWS, 256), 0)
    for h in range(HEADS):
        parts = [p[:, h * 80 : h * 80 + 80] for p in projected]
        block = jnp.concatenate(parts + [jnp.zeros((ROWS, 16), F32)], axis=1)
        block = jnp.where(slot_row >= CAP, count, block)
        heads[h] = block.astype(BF16)

    pl.semaphore_wait(barrier, len(peers))
    up_head = ((y + 1) % 4) * 2
    down_head = ((y + 3) % 4) * 2 + 1
    from_down = send("qkv+", heads.at[up_head], other.at[0], at_y(1))
    from_up = send("qkv-", heads.at[down_head], other.at[1], at_y(-1))

    lane = iota((ROWS, 128), 1)
    slot128 = iota((ROWS, 128), 0).astype(F32)

    def make_query(block, j, first):
        window = pltpu.roll(block[:, 128:256].astype(F32), 96, 1)
        query = jnp.where(lane < 80, window, jnp.where(lane == 80, 1.0, 0.0))
        qx[j, first : first + ROWS, :] = query.astype(BF16)

    lane88 = iota((ROWS // 2, 128), 1)

    def fold(first, second, part):
        both = jnp.concatenate(
            [first[:, 0:160].astype(F32), second[:, 0:160].astype(F32), jnp.zeros((ROWS, 64), F32)],
            axis=1,
        )
        third = both[:, 256:384]
        third = jnp.where(lane88 < 64, third[0:88], pltpu.roll(third[88:ROWS], 64, 1))
        part[0:ROWS, :] = both[:, 0:128].astype(BF16)
        part[ROWS : 2 * ROWS, :] = both[:, 128:256].astype(BF16)
        third = jnp.concatenate([third, jnp.zeros((8, 128), F32)], axis=0)
        part[2 * ROWS : PART, :] = third.astype(BF16)

    def unfold(part, first):
        p0 = part[0:ROWS, :].astype(F32)
        p1 = part[ROWS : 2 * ROWS, :].astype(F32)
        third = part[2 * ROWS : PART, :].astype(F32)[0:88]
        p2 = jnp.concatenate([third, pltpu.roll(third, 64, 1)], axis=0)
        pairs = (
            (p0, pltpu.roll(jnp.concatenate([p0, p1], axis=1), 176, 1)),
            (pltpu.roll(p1, 96, 1), pltpu.roll(jnp.concatenate([p1, p2], axis=1), 144, 1)),
        )
        for j in range(2):
            key, value = pairs[j]
            counts = key[CAP : CAP + 1, :]
            outside = jnp.where((lane == 80) & (slot128 >= counts), OUT_MASK, 0.0)
            keys[j, first : first + ROWS, :] = jnp.where(lane < 80, key, outside).astype(BF16)
            vals[j, first : first + ROWS, :] = jnp.where(
                lane == 80, 1.0, value[:, 0:128]
            ).astype(BF16)

    ring = {}

    def ring_start(part):
        ring["r", part, 0] = send("r0%d" % part, kv_own.at[part], kv_r.at[part, 0], at_z(1))
        ring["l", part, 0] = send("l0%d" % part, kv_own.at[part], kv_l.at[part, 0], at_z(-1))

    def ring_next(part, step):
        for way, buffer, to in (("r", kv_r, 1), ("l", kv_l, -1)):
            ring[way, part, step].wait_recv()
            if step < 2 or (step == 2 and (way == "r") == (part == 0)):
                ring[way, part, step + 1] = send(
                    "%s%d%d" % (way, step + 1, part),
                    buffer.at[part, step],
                    buffer.at[part, step + 1],
                    at_z(to),
                )

    own = [heads[y * 2], heads[y * 2 + 1]]
    fold(own[0], own[1], kv_own.at[0])
    ring_start(0)
    for j in range(2):
        make_query(own[j], j, 0)
    from_down.wait_recv()
    from_up.wait_recv()
    others = [other[0], other[1]]
    fold(others[0], others[1], kv_own.at[1])
    ring_start(1)
    for j in range(2):
        make_query(others[j], j, ROWS)

    scale = math.log2(math.e) / math.sqrt(HEAD_DIM)

    def attend_head(j, first, begin=False):
        span = slice(first, first + 2 * ROWS)
        scores = dot_nt(qx[j], keys[j, span, :])
        best = jnp.max(scores, axis=1, keepdims=True)
        if not begin:
            before = top[j]
            best = jnp.maximum(before[:, 0:1], best)
        probs = jnp.exp2((scores - best) * scale).astype(BF16)
        term = dot(probs, vals[j, span, :])
        if not begin:
            term = term + acc[j] * jnp.exp2((before - best) * scale)
        acc[j] = term
        top[j] = jnp.broadcast_to(best, (2 * ROWS, 128))

    def attend(first, one, two, begin=False):
        unfold(one, first)
        unfold(two, first + ROWS)
        for j in range(2):
            attend_head(j, first, begin)

    grad_scale = 8.0 / math.sqrt(8 * 16 * (TILE - VIS_TILE))
    root_half = 1.0 / math.sqrt(2.0)
    order = iota((DEC, DEC), 1)
    source = (order // 32 % 4) * 128 + (order // 256) * 64 + (order // 128 % 2) * 32 + order % 32
    shuffle = (iota((DEC, DEC), 0) == source).astype(F32).astype(BF16)

    def decode_forward(stream, goal, keep, unit, act, ready):
        normal, inverse = normalize(stream)
        low = normal.astype(BF16)
        unit[...] = low
        hidden = dot(low, wup[...])
        cumulative = 0.5 * (1.0 + lax.erf(hidden * root_half))
        active = (hidden * cumulative).astype(BF16)
        act[...] = active
        ready()
        slope = cumulative + hidden * jnp.exp(-0.5 * hidden * hidden) * (
            1.0 / math.sqrt(2.0 * math.pi)
        )
        stream_out = stream + dot(active, wdown[...])
        predicted = dot_nt(stream_out.astype(BF16), whead[...])
        pred_grad = ((predicted - goal) * (keep * grad_scale)).astype(BF16)
        out_grad = dot(pred_grad, whead[...])
        return normal, inverse, slope, out_grad

    def decode_hidden(out_low, slope, hg):
        hidden_grad = (dot_nt(out_low, wdown[...]) * slope).astype(BF16)
        for c in range(2):
            for px in range(4):
                at = px * 256 + c * 128
                hg[c, :, px * 128 : px * 128 + 128] = hidden_grad[:, at : at + 128]
        return hidden_grad

    def split_out(out_low, og):
        mixed = dot(out_low, shuffle).astype(BF16)
        og[0] = mixed[:, 0:256]
        og[1] = mixed[:, 256:512]

    attend(0, kv_own.at[0], kv_own.at[1], begin=True)
    for name in ("dpos", "targets", "wup", "wdown", "whead"):
        loads[name].wait()
    ring_next(0, 0)
    part_rows = pl.ds(pl.multiple_of(seg * HALF, 16), HALF)
    stream_m = mtok_ref[...].astype(F32)[None, :] + dpos[part_rows, :].astype(F32)
    patch = iota((HALF, TILE), 0) + seg * HALF
    pick = (iota((HALF, TILE), 1) == patch).astype(F32).astype(BF16)
    goal_m = dot_nt(pick, targets[...])
    keep_m = 1.0 - seen_col[part_rows, :][:, 0:1]
    masked = []

    def ready_m():
        masked.append(send("unit_m", unit_m, unit_ms, sibling))
        masked.append(send("act_m", act_m, act_ms, sibling))
        ring_next(1, 0)

    normal, inverse, slope, out_grad = decode_forward(
        stream_m, goal_m, keep_m, unit_m, act_m, ready_m
    )
    attend(2 * ROWS, kv_r.at[0, 0], kv_l.at[0, 0])
    ring_next(0, 1)
    out_low = out_grad.astype(BF16)
    split_out(out_low, og_m)
    masked.append(send("og_m", og_m.at[1 - core], og_ms, sibling))
    decode_hidden(out_low, slope, hg_m)
    masked.append(send("hg_m", hg_m.at[1 - core], hg_ms, sibling))
    attend(4 * ROWS, kv_r.at[1, 0], kv_l.at[1, 0])
    ring_next(1, 1)
    attend(6 * ROWS, kv_r.at[0, 1], kv_l.at[0, 1])
    slot_first = pl.multiple_of(seg * SEG_STEP, 16)
    slot_rows = pl.ds(slot_first, SLOTS)
    chosen_part = selector[slot_rows, :]
    pos_slot[...] = dot(chosen_part, dpos[...])
    tgt_slot[...] = dot_nt(chosen_part, targets[...])
    number = iota((SLOTS, 128), 0) + seg * SEG_STEP
    kept = (number.astype(F32) < count) & (number >= seg * SLOTS)
    mask_slot[...] = jnp.where(kept, 1.0, 0.0)
    ring_next(0, 2)
    attend(8 * ROWS, kv_r.at[1, 1], kv_l.at[1, 1])
    for copy in masked:
        copy.wait_recv()
    gd_acc[...] = dot_tn(og_m[core], act_m[...]) + dot_tn(og_ms[...], act_ms[...])
    ring_next(1, 2)
    attend(10 * ROWS, kv_r.at[0, 2], kv_l.at[0, 2])
    gu_acc[...] = dot_tn(unit_m[...], hg_m[core]) + dot_tn(unit_ms[...], hg_ms[...])
    attend(12 * ROWS, kv_r.at[1, 2], kv_l.at[1, 2])
    loads["wout"].wait()
    loads["wembed"].wait()
    ring["r", 0, 3].wait_recv()
    ring["l", 1, 3].wait_recv()
    unfold(kv_r.at[0, 3], 14 * ROWS)
    unfold(kv_l.at[1, 3], 15 * ROWS)

    back = []
    for j in range(2):
        attend_head(j, 14 * ROWS)
        total = acc[j]
        done = (total * (1.0 / total[:, 80:81])).astype(BF16)
        att_out[j, 0] = done[0:ROWS]
        att_out[j, 1] = done[ROWS : 2 * ROWS]
        for step, i in ((2, 0), (1, 1), (-1, 1)):
            goal_seg = ((y + step + 4) % 4) // 2
            span = pl.ds(pl.multiple_of(goal_seg * SEG_STEP, 16), SLOTS)
            back.append(
                send("b%d%d" % (j, step + 4), att_out.at[j, i, span], att_in.at[y, j], at_y(step))
            )
        att_in[y, j] = att_out[j, 0, slot_rows, :]
    for copy in back:
        copy.wait_recv()
    pieces = [att_in[i // 2, i % 2][:, 0:80].astype(F32) for i in range(HEADS)]
    for c in range(2):
        att[c] = jnp.concatenate(pieces[c * 4 : c * 4 + 4], axis=1).astype(BF16)
    swap_att = send("att_s", att.at[1 - core], att_sib, sibling)
    attended = jnp.concatenate(pieces, axis=1).astype(BF16)

    encoded = packed[slot_rows, :].astype(F32) + dot(attended, wout[...])
    embedded = dot(encoded.astype(BF16), wembed[...])
    stream_v = embedded + pos_slot[...]
    swap = {}

    def ready_v():
        swap["unit"] = send("unit_v", unit_v, unit_vs, sibling)
        swap["act"] = send("act_v", act_v, act_vs, sibling)

    normal, inverse, slope, out_grad = decode_forward(
        stream_v, tgt_slot[...], mask_slot[:, 0:1], unit_v, act_v, ready_v
    )
    out_low = out_grad.astype(BF16)
    split_out(out_low, og_v)
    swap["og"] = send("og_v", og_v.at[1 - core], og_vs, sibling)
    hidden_grad = decode_hidden(out_low, slope, hg_v)
    swap["hg"] = send("hg_v", hg_v.at[1 - core], hg_vs, sibling)

    def ring_sum(name, chunks, landing, h0, h1, place, at):
        right, left, far = (place + 1) % 4, (place + 3) % 4, (place + 2) % 4
        s0, s1 = pl.ds(0, h0), pl.ds(h0, h1)
        rel0 = send(name + "rel0", chunks.at[far, s0], landing.at[0, s0], at(1))
        rel1 = send(name + "rel1", chunks.at[far, s1], landing.at[0, s1], at(-1))
        dir1 = send(name + "dir1", chunks.at[right, s1], landing.at[1, s1], at(1))
        dir0 = send(name + "dir0", chunks.at[left, s0], landing.at[1, s0], at(-1))
        state = {}

        def relay():
            rel0.wait_recv()
            landing[3, s0, :] = (
                landing[0, s0, :].astype(F32) + chunks[right, s0, :].astype(F32)
            ).astype(BF16)
            state["c0"] = send(name + "c0", landing.at[3, s0], landing.at[2, s0], at(1))
            rel1.wait_recv()
            landing[3, s1, :] = (
                landing[0, s1, :].astype(F32) + chunks[left, s1, :].astype(F32)
            ).astype(BF16)
            state["c1"] = send(name + "c1", landing.at[3, s1], landing.at[2, s1], at(-1))

        def finish():
            dir0.wait_recv()
            dir1.wait_recv()
            state["c0"].wait_recv()
            state["c1"].wait_recv()
            return (
                chunks[place].astype(F32) + landing[1].astype(F32) + landing[2].astype(F32)
            )

        return relay, finish

    swap["act"].wait_recv()
    swap["og"].wait_recv()
    gd_t = gd_acc[...] + dot_tn(og_v[core], act_v[...]) + dot_tn(og_vs[...], act_vs[...])
    gd_t = gd_t.astype(BF16)
    for py in range(4):
        for px in range(4):
            for k in range(4):
                r = (py // 2) * 128 + px * 32
                c = (py % 2) * 512 + k * 128
                at = px * 128 + k * 32
                rs_gd[py, at : at + 32, :] = gd_t[r : r + 32, c : c + 128]
    relay_gd, finish_gd = ring_sum("gd", rs_gd, in_gd, 256, 256, y, at_y)

    unit_grad = dot_nt(hidden_grad, wup[...])
    cross = jnp.mean(unit_grad * normal, axis=-1, keepdims=True)
    middle = jnp.mean(unit_grad, axis=-1, keepdims=True)
    stream_grad = out_grad + inverse * (unit_grad - middle - normal * cross)
    sg_v[...] = stream_grad.astype(BF16)
    swap["sg"] = send("sg_v", sg_v, sg_vs, sibling)

    swap["unit"].wait_recv()
    swap["hg"].wait_recv()
    gu_t = gu_acc[...] + dot_tn(unit_v[...], hg_v[core]) + dot_tn(unit_vs[...], hg_vs[...])
    gu_t = gu_t.astype(BF16)
    for px in range(4):
        rs_gu[px] = gu_t[:, px * 128 : px * 128 + 128]
    relay_gu, finish_gu = ring_sum("gu", rs_gu, in_gu, 256, 256, x, at_x)

    swap_att.wait_recv()
    swap["sg"].wait_recv()
    inner = dot_tn(att[core], sg_v[...]) + dot_tn(att_sib[...], sg_vs[...])
    inner = inner.astype(BF16)
    for px in range(4):
        for i in range(4):
            rs_g[px, 48 * i : 48 * i + 48, :] = inner[80 * i : 80 * i + 48, px * 128 : px * 128 + 128]
            rs_h[i, 32 * px : 32 * px + 32, :] = inner[
                80 * i + 48 : 80 * i + 80, px * 128 : px * 128 + 128
            ]
    relay_g, finish_g = ring_sum("g", rs_g, in_g, 96, 96, x, at_x)
    relay_h, finish_h = ring_sum("h", rs_h, in_h, 64, 64, y, at_y)

    relay_gd()
    relay_gu()
    relay_g()
    relay_h()

    gd_1 = finish_gd()
    h_1 = finish_h()
    for px in range(4):
        rs_y2[px, 0:128, :] = gd_1[px * 128 : px * 128 + 128].astype(BF16)
        rs_y2[px, 128:160, :] = h_1[px * 32 : px * 32 + 32].astype(BF16)
    relay_y2, finish_y2 = ring_sum("y2", rs_y2, in_y2, 80, 80, x, at_x)
    gu_1 = finish_gu()
    g_1 = finish_g()
    lane128 = iota((128, 128), 1)
    for py in range(4):
        first = gu_1[(py % 2) * 256 : (py % 2) * 256 + 128]
        second = gu_1[(py % 2) * 256 + 128 : (py % 2) * 256 + 256]
        if py // 2 == 0:
            pair = jnp.where(lane128 < 64, first, pltpu.roll(second, 64, 1))
        else:
            pair = jnp.where(lane128 < 64, pltpu.roll(first, 64, 1), second)
        rs_x2[py, 0:128, :] = pair.astype(BF16)
        rs_x2[py, 128:176, :] = g_1[py * 48 : py * 48 + 48].astype(BF16)
    relay_x2, finish_x2 = ring_sum("x2", rs_x2, in_x2, 96, 80, y, at_y)
    relay_y2()
    relay_x2()
    y_2 = finish_y2()
    x_2 = finish_x2()

    zg[0] = x_2[128:176].astype(BF16)
    zg[1] = jnp.concatenate([x_2[160:176], y_2[128:160]], axis=0).astype(BF16)
    holder = z // 2 == y
    inner_copies = []
    for step in range(1, 8):
        to = (z + step) % 8
        copy = describe("zg%d" % step, zg.at[to % 2], zgr.at[step - 1], at_z(step))
        goes = to // 2 == y
        pl.when(goes)(copy.start)
        inner_copies.append((copy, goes))
    lane32 = iota((32, 128), 1)
    for pz in range(8):
        up = x_2[(pz % 4) * 32 : (pz % 4) * 32 + 32]
        if pz // 4 == 1:
            up = pltpu.roll(up, 64, 1)
        down = y_2[(pz // 2) * 32 : (pz // 2) * 32 + 32]
        if pz % 2 == 0:
            down = pltpu.roll(down, 64, 1)
        zs[pz] = jnp.where(lane32 < 64, up, down).astype(BF16)
    last = []
    for step in range(1, 8):
        last.append(send("z%d" % step, zs.at[(z + step) % 8], zr.at[step - 1], at_z(step)))

    spread = []
    for step in range(4):
        for pc in range(2):
            for half in range(2):
                target = device((x + step) % 4, pc, core + 2 * half, z)
                copy = describe("ag%d%d%d" % (step, pc, half), ag, gr.at[x], target, "ag%d" % step)
                goes = holder
                if step == 0:
                    goes = holder & ((core != pc) | (y != core + 2 * half))
                spread.append((copy, goes))

    @pl.when(holder)
    def _():
        total = zg[z % 2].astype(F32)
        for step in range(1, 8):
            inner_copies[step - 1][0].wait_recv()
            total = total + zgr[step - 1].astype(F32)
        ag[...] = total.astype(BF16)

    for copy, goes in spread:
        pl.when(goes)(copy.start)
    mine = holder & (core == y_lo)

    @pl.when(mine)
    def _():
        gr[x] = ag[...]

    result = zs[z].astype(F32)
    for step in range(1, 8):
        last[step - 1].wait_recv()
        result = result + zr[step - 1].astype(F32)
    sums_ref[0:32, :] = result
    pl.when(jnp.logical_not(mine))(spread[0][0].wait_recv)
    for step in range(1, 4):
        spread[step * 4][0].wait_recv()
    rows_b = jnp.concatenate([gr[i] for i in range(4)], axis=1)
    columns = pl.ds(pl.multiple_of((x * 4 + core * 2 + seg) * 80, 16), 80)
    product = dot_nt(rows_b, wembed[columns, :])
    product = jnp.where(z % 2 == 0, product[0:40], product[8:48])
    sums_ref[32:72, 0:80] = product
    for copy, goes in inner_copies + spread:
        pl.when(goes)(copy.wait_send)
    for copy in started:
        copy.wait_send()


def split_sums(sums_ref, go_ref, gu_ref, gd_ref):
    go_ref[...] = sums_ref[32:72, 0:80]
    gu_ref[...] = sums_ref[0:32, 0:64]
    gd_ref[...] = pltpu.roll(sums_ref[0:32, :], 64, 1)[:, 0:64]


def on_device(
    tokens, targets, visible, w_qkv, w_out, w_embed, mask_token, dec_pos, w_up, w_down, w_head
):
    names.clear()
    anywhere = pl.BlockSpec(memory_space=pl.ANY)
    vmem = pl.BlockSpec(memory_space=pltpu.VMEM)

    def low(*shape):
        return pltpu.VMEM(shape, BF16)

    def wide(*shape):
        return pltpu.VMEM(shape, F32)

    scratch = [
        low(TILE, D), low(PIX, TILE), low(D, INNER), low(D, INNER), low(D, INNER), low(INNER, D),
        low(D, DEC), low(TILE, DEC), low(DEC, FF), low(FF, DEC), low(PIX, DEC),
        low(ROWS, TILE), wide(TILE, 128), low(ROWS, D), low(HEADS, ROWS, 256), low(2, ROWS, 256),
        low(2, PART, 128), low(2, 4, PART, 128), low(2, 4, PART, 128),
        low(2, 16 * ROWS, 128), low(2, 16 * ROWS, 128), low(2, 2 * ROWS, 128),
        wide(2, 2 * ROWS, 128), wide(2, 2 * ROWS, 128),
        low(2, 2, ROWS, 128), low(4, 2, SLOTS, 128), low(2, SLOTS, 320), low(SLOTS, 320),
        wide(SLOTS, DEC), wide(SLOTS, PIX), wide(SLOTS, 128),
        low(HALF, DEC), low(HALF, FF), low(2, HALF, 256), low(2, HALF, DEC),
        low(HALF, DEC), low(HALF, FF), low(HALF, 256), low(HALF, DEC),
        wide(256, FF), wide(DEC, DEC),
        low(SLOTS, DEC), low(SLOTS, FF), low(2, SLOTS, 256), low(2, SLOTS, DEC), low(SLOTS, DEC),
        low(SLOTS, DEC), low(SLOTS, FF), low(SLOTS, 256), low(SLOTS, DEC), low(SLOTS, DEC),
        low(4, 512, 128), low(4, 512, 128), low(4, 192, 128), low(4, 128, 128),
        low(4, 176, 128), low(4, 160, 128),
        low(4, 512, 128), low(4, 512, 128), low(4, 192, 128), low(4, 128, 128),
        low(4, 176, 128), low(4, 160, 128),
        low(8, 32, 128), low(7, 32, 128), low(2, 48, 128), low(7, 48, 128), low(48, 128),
        low(4, 48, 128),
        pltpu.SemaphoreType.DMA((N_REMOTE,)),
        pltpu.SemaphoreType.DMA((N_REMOTE,)),
        pltpu.SemaphoreType.DMA((N_LOCAL,)),
    ]
    sums = pl.pallas_call(
        kernel,
        out_shape=jax.ShapeDtypeStruct((80, 128), F32),
        in_specs=[
            anywhere, anywhere, vmem, anywhere, anywhere, anywhere, vmem, anywhere, anywhere,
            anywhere, anywhere,
        ],
        out_specs=vmem,
        scratch_shapes=scratch,
        compiler_params=pltpu.CompilerParams(
            collective_id=0, has_side_effects=True, vmem_limit_bytes=56 * 1024 * 1024
        ),
    )(
        tokens[0], targets[0].T, visible, w_qkv, w_out, w_embed, mask_token, dec_pos, w_up,
        w_down, w_head.T,
    )
    grad_out, grad_up, grad_down = pl.pallas_call(
        split_sums,
        out_shape=(
            jax.ShapeDtypeStruct((40, 80), F32),
            jax.ShapeDtypeStruct((32, 64), F32),
            jax.ShapeDtypeStruct((32, 64), F32),
        ),
        in_specs=[vmem],
        out_specs=(vmem, vmem, vmem),
    )(sums)
    return grad_out, grad_up, grad_down.T


def solution(mesh):
    in_specs = (
        P("dp", "blk", None),
        P("dp", "blk", None),
        P("dp", "blk"),
        P(),
        P(),
        P(),
        P(),
        P("blk", None),
        P(),
        P(),
        P(),
    )
    out_specs = (
        P("blk", ("dp", "segment")),
        P("blk", ("dp", "segment")),
        P("blk", ("dp", "segment")),
    )
    return jax.shard_map(
        on_device, mesh=mesh, in_specs=in_specs, out_specs=out_specs, check_vma=False
    )
```

```python
import math

import jax
import jax.numpy as jnp
from jax import lax
from jax.experimental import pallas as pl
from jax.experimental.pallas import tpu as pltpu
from jax.sharding import PartitionSpec as P

MESH = pl.DeviceIdType.MESH
F32 = jnp.float32
BF16 = jnp.bfloat16

HEADS = 8
HEAD_DIM = 80
VIS_TILE = 96
TILE = 384
CAP = 168
ROWS = 176
D = 1280
DEC = 512
FF = 1024
PIX = 1176
INNER = 640
HALF = 192
SLOTS = 96
SEG_STEP = 80
PART = 448
EPS = 1e-05
OUT_MASK = -1e30


def dot(a, b):
    return lax.dot_general(a, b, (((1,), (0,)), ((), ())), preferred_element_type=F32)


def dot_nt(a, b):
    return lax.dot_general(a, b, (((1,), (1,)), ((), ())), preferred_element_type=F32)


def dot_tn(a, b):
    return lax.dot_general(a, b, (((0,), (0,)), ((), ())), preferred_element_type=F32)


def normalize(rows):
    center = rows - jnp.mean(rows, axis=-1, keepdims=True)
    inverse = lax.rsqrt(jnp.mean(center * center, axis=-1, keepdims=True) + EPS)
    return center * inverse, inverse


def iota(shape, axis):
    return lax.broadcasted_iota(jnp.int32, shape, axis)


names = []


def ident(name):
    if name not in names:
        names.append(name)
    return names.index(name)


N_SEND = 32
N_RECV = 88
N_LOCAL = 14


def kernel(
    tokens_h, targets_h, vis_ref, wqkv_h, wout_h, wembed_h, mtok_ref, dpos_h, wup_h, wdown_h, whead_h,
    sums_ref,
    tokens, targets, wq, wk, wv, wout, wembed, dpos, wup, wdown, whead,
    selector, seen_col, packed, heads, other, kv_own, kv_r, kv_l, keys, vals, qx, acc, top,
    att_out, att_in, att, att_sib, pos_slot, tgt_slot, mask_slot,
    unit_m, act_m, og_m, hg_m, unit_ms, act_ms, og_ms, hg_ms, gd_acc, gu_acc,
    unit_v, act_v, og_v, hg_v, sg_v, unit_vs, act_vs, og_vs, hg_vs, sg_vs,
    rs_gd, rs_gu, rs_g, rs_h, rs_gd2, rs_gu2, rs_g2, rs_h2,
    in_gd, in_gu, in_g, in_h, in_gd2, in_gu2, in_g2, in_h2,
    zs, zr, zg, zgr, ag, gr,
    send_sem, recv_sem, load_sem,
):
    dp = lax.axis_index("dp")
    seg = lax.axis_index("segment")
    blk = lax.axis_index("blk")
    x, core = dp // 2, dp % 2
    y, z = seg * 2 + blk // 8, blk % 8
    y_lo = blk // 8

    def device(px, pc, py, pz):
        return (px * 2 + pc, py // 2, (py % 2) * 8 + pz)

    def at_x(step):
        return device((x + step + 4) % 4, core, y, z)

    def at_y(step):
        return device(x, core, (y + step + 4) % 4, z)

    def at_z(step):
        return device(x, core, y, (z + step + 8) % 8)

    sibling = device(x, 1 - core, y, z)

    loads = {}

    def load(name, src, dst):
        copy = pltpu.make_async_copy(src, dst, load_sem.at[len(loads)])
        copy.start()
        loads[name] = copy

    load("tokens", tokens_h, tokens)
    for name, dst, first in (("wk", wk, 640), ("wv", wv, 1280), ("wq", wq, 0)):
        for part in range(2):
            span = pl.ds(part * 640, 640)
            load(name + str(part), wqkv_h.at[span, pl.ds(first, 640)], dst.at[span])

    barrier = pltpu.get_barrier_semaphore()
    holder = z // 2 == y
    mine = holder & (core == y_lo)
    peers = [sibling] + [at_z(step) for step in range(1, 8)]
    peers += [at_x(step) for step in range(1, 4)] + [at_y(step) for step in range(1, 4)]
    for peer in peers:
        pl.semaphore_signal(barrier, inc=1, device_id=peer, device_id_type=MESH)
    for step in range(4):
        source = device((x + step) % 4, y_lo, z // 2, z)

        def greet():
            pl.semaphore_signal(barrier, inc=1, device_id=source, device_id_type=MESH)

        if step == 0:
            pl.when(jnp.logical_not(mine))(greet)
        else:
            greet()
    greetings = len(peers) + jnp.where(holder, 16, 0) - jnp.where(mine, 1, 0)

    started = []

    def describe(src, dst, target, slot, name):
        return pltpu.make_async_remote_copy(
            src_ref=src,
            dst_ref=dst,
            send_sem=send_sem.at[slot],
            recv_sem=recv_sem.at[ident(name)],
            device_id=target,
            device_id_type=MESH,
        )

    def send(name, src, dst, target):
        count = len(started)
        if count >= N_SEND:
            started[count - N_SEND].wait_send()
        copy = describe(src, dst, target, count % N_SEND, name)
        copy.start()
        started.append(copy)
        return copy

    vis = vis_ref[...].astype(F32)
    tri = (iota((TILE, TILE), 0) <= iota((TILE, TILE), 1)).astype(F32).astype(BF16)
    vis8 = jnp.broadcast_to(vis, (8, TILE))
    position = dot(vis8.astype(BF16), tri)[0:1, :] - 1.0
    count = jnp.sum(vis, axis=1, keepdims=True)
    slot_ids = iota((ROWS, TILE), 0).astype(F32)
    chosen = jnp.where((position == slot_ids) & (vis > 0.5), 1.0, 0.0).astype(BF16)
    selector[...] = chosen
    loads["tokens"].wait()
    rows = dot(chosen, tokens[...])
    packed[...] = rows.astype(BF16)
    normed = normalize(rows)[0].astype(BF16)
    seen_col[...] = dot_tn(chosen, jnp.ones((ROWS, 128), BF16))
    projected = []
    for name, weight in (("wk", wk), ("wv", wv), ("wq", wq)):
        loads[name + "0"].wait()
        loads[name + "1"].wait()
        projected.append(dot(normed, weight[...]))
    load("dpos", dpos_h, dpos)
    load("targets", targets_h, targets)
    load("wup", wup_h, wup)
    load("wdown", wdown_h, wdown)
    load("whead", whead_h, whead)
    load("wout", wout_h, wout)
    load("wembed", wembed_h, wembed)
    slot_row = iota((ROWS, 256), 0)
    for h in range(HEADS):
        parts = [p[:, h * 80 : h * 80 + 80] for p in projected]
        block = jnp.concatenate(parts + [jnp.zeros((ROWS, 16), F32)], axis=1)
        block = jnp.where(slot_row >= CAP, count, block)
        heads[h] = block.astype(BF16)

    pl.semaphore_wait(barrier, greetings)
    up_head = ((y + 1) % 4) * 2
    down_head = ((y + 3) % 4) * 2 + 1
    from_down = send("qkv+", heads.at[up_head], other.at[0], at_y(1))
    from_up = send("qkv-", heads.at[down_head], other.at[1], at_y(-1))

    lane = iota((ROWS, 128), 1)
    slot128 = iota((ROWS, 128), 0).astype(F32)

    def make_query(block, j, first):
        window = pltpu.roll(block[:, 128:256].astype(F32), 96, 1)
        query = jnp.where(lane < 80, window, jnp.where(lane == 80, 1.0, 0.0))
        qx[j, first : first + ROWS, :] = query.astype(BF16)

    lane88 = iota((ROWS // 2, 128), 1)

    def fold(first, second, part):
        both = jnp.concatenate(
            [first[:, 0:160].astype(F32), second[:, 0:160].astype(F32), jnp.zeros((ROWS, 64), F32)],
            axis=1,
        )
        third = both[:, 256:384]
        third = jnp.where(lane88 < 64, third[0:88], pltpu.roll(third[88:ROWS], 64, 1))
        part[0:ROWS, :] = both[:, 0:128].astype(BF16)
        part[ROWS : 2 * ROWS, :] = both[:, 128:256].astype(BF16)
        third = jnp.concatenate([third, jnp.zeros((8, 128), F32)], axis=0)
        part[2 * ROWS : PART, :] = third.astype(BF16)

    def unfold(part, first):
        p0 = part[0:ROWS, :].astype(F32)
        p1 = part[ROWS : 2 * ROWS, :].astype(F32)
        third = part[2 * ROWS : PART, :].astype(F32)[0:88]
        p2 = jnp.concatenate([third, pltpu.roll(third, 64, 1)], axis=0)
        pairs = (
            (p0, pltpu.roll(jnp.concatenate([p0, p1], axis=1), 176, 1)),
            (pltpu.roll(p1, 96, 1), pltpu.roll(jnp.concatenate([p1, p2], axis=1), 144, 1)),
        )
        for j in range(2):
            key, value = pairs[j]
            counts = key[CAP : CAP + 1, :]
            outside = jnp.where((lane == 80) & (slot128 >= counts), OUT_MASK, 0.0)
            keys[j, first : first + ROWS, :] = jnp.where(lane < 80, key, outside).astype(BF16)
            vals[j, first : first + ROWS, :] = jnp.where(
                lane == 80, 1.0, value[:, 0:128]
            ).astype(BF16)

    ring = {}
    ring_halves = (pl.ds(0, PART // 2), pl.ds(PART // 2, PART // 2))

    def ring_send(way, part, step, half, src):
        buffer, to = (kv_r, 1) if way == "r" else (kv_l, -1)
        rows_of = ring_halves[half]
        ring[way, part, step, half] = send(
            "%s%d%d%d" % (way, step, part, half),
            src.at[rows_of],
            buffer.at[part, step, rows_of],
            at_z(to),
        )

    def ring_start(part):
        for half in range(2):
            for way in "rl":
                ring_send(way, part, 0, half, kv_own.at[part])

    def ring_next(part, step):
        for half in range(2):
            for way, buffer in (("r", kv_r), ("l", kv_l)):
                ring[way, part, step, half].wait_recv()
                if step < 2 or (step == 2 and (way == "r") == (part == 0)):
                    ring_send(way, part, step + 1, half, buffer.at[part, step])

    own = [heads[y * 2], heads[y * 2 + 1]]
    fold(own[0], own[1], kv_own.at[0])
    ring_start(0)
    for j in range(2):
        make_query(own[j], j, 0)
    from_down.wait_recv()
    from_up.wait_recv()
    others = [other[0], other[1]]
    fold(others[0], others[1], kv_own.at[1])
    ring_start(1)
    for j in range(2):
        make_query(others[j], j, ROWS)

    scale = math.log2(math.e) / math.sqrt(HEAD_DIM)

    def attend_head(j, first, begin=False):
        span = slice(first, first + 2 * ROWS)
        scores = dot_nt(qx[j], keys[j, span, :])
        best = jnp.max(scores, axis=1, keepdims=True)
        if not begin:
            before = top[j]
            best = jnp.maximum(before[:, 0:1], best)
        probs = jnp.exp2((scores - best) * scale).astype(BF16)
        term = dot(probs, vals[j, span, :])
        if not begin:
            term = term + acc[j] * jnp.exp2((before - best) * scale)
        acc[j] = term
        top[j] = jnp.broadcast_to(best, (2 * ROWS, 128))

    def attend(first, one, two, begin=False):
        unfold(one, first)
        unfold(two, first + ROWS)
        for j in range(2):
            attend_head(j, first, begin)

    grad_scale = 8.0 / math.sqrt(8 * 16 * (TILE - VIS_TILE))
    root_half = 1.0 / math.sqrt(2.0)
    order = iota((DEC, DEC), 1)
    source = (order // 32 % 4) * 128 + (order // 256) * 64 + (order // 128 % 2) * 32 + order % 32
    shuffle = (iota((DEC, DEC), 0) == source).astype(F32).astype(BF16)

    def decode_forward(stream, goal, keep, unit, act, ready):
        normal, inverse = normalize(stream)
        low = normal.astype(BF16)
        unit[...] = low
        hidden = dot(low, wup[...])
        cumulative = 0.5 * (1.0 + lax.erf(hidden * root_half))
        active = (hidden * cumulative).astype(BF16)
        act[...] = active
        ready()
        slope = cumulative + hidden * jnp.exp(-0.5 * hidden * hidden) * (
            1.0 / math.sqrt(2.0 * math.pi)
        )
        stream_out = stream + dot(active, wdown[...])
        predicted = dot_nt(stream_out.astype(BF16), whead[...])
        pred_grad = ((predicted - goal) * (keep * grad_scale)).astype(BF16)
        out_grad = dot(pred_grad, whead[...])
        return normal, inverse, slope, out_grad

    def decode_hidden(out_low, slope, hg):
        hidden_grad = (dot_nt(out_low, wdown[...]) * slope).astype(BF16)
        for c in range(2):
            for px in range(4):
                at = px * 256 + c * 128
                hg[c, :, px * 128 : px * 128 + 128] = hidden_grad[:, at : at + 128]
        return hidden_grad

    def split_out(out_low, og):
        mixed = dot(out_low, shuffle).astype(BF16)
        og[0] = mixed[:, 0:256]
        og[1] = mixed[:, 256:512]

    attend(0, kv_own.at[0], kv_own.at[1], begin=True)
    for name in ("dpos", "targets", "wup", "wdown", "whead"):
        loads[name].wait()
    ring_next(0, 0)
    part_rows = pl.ds(pl.multiple_of(seg * HALF, 16), HALF)
    stream_m = mtok_ref[...].astype(F32)[None, :] + dpos[part_rows, :].astype(F32)
    patch = iota((HALF, TILE), 0) + seg * HALF
    pick = (iota((HALF, TILE), 1) == patch).astype(F32).astype(BF16)
    goal_m = dot_nt(pick, targets[...])
    keep_m = 1.0 - seen_col[part_rows, :][:, 0:1]
    masked = []

    def ready_m():
        masked.append(send("unit_m", unit_m, unit_ms, sibling))
        masked.append(send("act_m", act_m, act_ms, sibling))
        ring_next(1, 0)

    normal, inverse, slope, out_grad = decode_forward(
        stream_m, goal_m, keep_m, unit_m, act_m, ready_m
    )
    attend(2 * ROWS, kv_r.at[0, 0], kv_l.at[0, 0])
    ring_next(0, 1)
    out_low = out_grad.astype(BF16)
    split_out(out_low, og_m)
    masked.append(send("og_m", og_m.at[1 - core], og_ms, sibling))
    decode_hidden(out_low, slope, hg_m)
    masked.append(send("hg_m", hg_m.at[1 - core], hg_ms, sibling))
    attend(4 * ROWS, kv_r.at[1, 0], kv_l.at[1, 0])
    ring_next(1, 1)
    attend(6 * ROWS, kv_r.at[0, 1], kv_l.at[0, 1])
    slot_first = pl.multiple_of(seg * SEG_STEP, 16)
    slot_rows = pl.ds(slot_first, SLOTS)
    chosen_part = selector[slot_rows, :]
    pos_slot[...] = dot(chosen_part, dpos[...])
    tgt_slot[...] = dot_nt(chosen_part, targets[...])
    number = iota((SLOTS, 128), 0) + seg * SEG_STEP
    kept = (number.astype(F32) < count) & (number >= seg * SLOTS)
    mask_slot[...] = jnp.where(kept, 1.0, 0.0)
    ring_next(0, 2)
    attend(8 * ROWS, kv_r.at[1, 1], kv_l.at[1, 1])
    for copy in masked:
        copy.wait_recv()
    gd_acc[...] = dot_tn(og_m[core], act_m[...]) + dot_tn(og_ms[...], act_ms[...])
    ring_next(1, 2)
    attend(10 * ROWS, kv_r.at[0, 2], kv_l.at[0, 2])
    gu_acc[...] = dot_tn(unit_m[...], hg_m[core]) + dot_tn(unit_ms[...], hg_ms[...])
    attend(12 * ROWS, kv_r.at[1, 2], kv_l.at[1, 2])
    loads["wout"].wait()
    loads["wembed"].wait()
    for half in range(2):
        ring["r", 0, 3, half].wait_recv()
        ring["l", 1, 3, half].wait_recv()
    unfold(kv_r.at[0, 3], 14 * ROWS)
    unfold(kv_l.at[1, 3], 15 * ROWS)

    back = []
    for j in range(2):
        attend_head(j, 14 * ROWS)
        total = acc[j]
        done = (total * (1.0 / total[:, 80:81])).astype(BF16)
        att_out[j, 0] = done[0:ROWS]
        att_out[j, 1] = done[ROWS : 2 * ROWS]
        for step, i in ((2, 0), (1, 1), (-1, 1)):
            goal_seg = ((y + step + 4) % 4) // 2
            span = pl.ds(pl.multiple_of(goal_seg * SEG_STEP, 16), SLOTS)
            back.append(
                send("b%d%d" % (j, step + 4), att_out.at[j, i, span], att_in.at[y, j], at_y(step))
            )
        att_in[y, j] = att_out[j, 0, slot_rows, :]
    for copy in back:
        copy.wait_recv()
    pieces = [att_in[i // 2, i % 2][:, 0:80].astype(F32) for i in range(HEADS)]
    for c in range(2):
        att[c] = jnp.concatenate(pieces[c * 4 : c * 4 + 4], axis=1).astype(BF16)
    swap_att = send("att_s", att.at[1 - core], att_sib, sibling)
    attended = jnp.concatenate(pieces, axis=1).astype(BF16)

    encoded = packed[slot_rows, :].astype(F32) + dot(attended, wout[...])
    embedded = dot(encoded.astype(BF16), wembed[...])
    stream_v = embedded + pos_slot[...]
    swap = {}

    def ready_v():
        swap["unit"] = send("unit_v", unit_v, unit_vs, sibling)
        swap["act"] = send("act_v", act_v, act_vs, sibling)

    normal, inverse, slope, out_grad = decode_forward(
        stream_v, tgt_slot[...], mask_slot[:, 0:1], unit_v, act_v, ready_v
    )
    out_low = out_grad.astype(BF16)
    split_out(out_low, og_v)
    swap["og"] = send("og_v", og_v.at[1 - core], og_vs, sibling)
    hidden_grad = decode_hidden(out_low, slope, hg_v)
    swap["hg"] = send("hg_v", hg_v.at[1 - core], hg_vs, sibling)

    def direct_sum(name, chunks, landing, place, at):
        copies = [
            send(name + str(step), chunks.at[(place + step) % 4], landing.at[step - 1], at(step))
            for step in range(1, 4)
        ]

        def finish():
            total = chunks[place].astype(F32)
            for step in range(3):
                copies[step].wait_recv()
                total = total + landing[step].astype(F32)
            return total

        return finish

    swap["act"].wait_recv()
    swap["og"].wait_recv()
    gd_t = gd_acc[...] + dot_tn(og_v[core], act_v[...]) + dot_tn(og_vs[...], act_vs[...])
    gd_t = gd_t.astype(BF16)
    for py in range(4):
        for px in range(4):
            for k in range(4):
                r = (py // 2) * 128 + px * 32
                c = (py % 2) * 512 + k * 128
                at = px * 128 + k * 32
                rs_gd[py, at : at + 32, :] = gd_t[r : r + 32, c : c + 128]
    finish_gd = direct_sum("gd", rs_gd, in_gd, y, at_y)

    unit_grad = dot_nt(hidden_grad, wup[...])
    cross = jnp.mean(unit_grad * normal, axis=-1, keepdims=True)
    middle = jnp.mean(unit_grad, axis=-1, keepdims=True)
    stream_grad = out_grad + inverse * (unit_grad - middle - normal * cross)
    sg_v[...] = stream_grad.astype(BF16)
    swap["sg"] = send("sg_v", sg_v, sg_vs, sibling)

    swap["unit"].wait_recv()
    swap["hg"].wait_recv()
    gu_t = gu_acc[...] + dot_tn(unit_v[...], hg_v[core]) + dot_tn(unit_vs[...], hg_vs[...])
    gu_t = gu_t.astype(BF16)
    for px in range(4):
        rs_gu[px] = gu_t[:, px * 128 : px * 128 + 128]

    swap_att.wait_recv()
    swap["sg"].wait_recv()
    inner = dot_tn(att[core], sg_v[...]) + dot_tn(att_sib[...], sg_vs[...])
    inner = inner.astype(BF16)
    for px in range(4):
        for i in range(4):
            rs_g[px, 48 * i : 48 * i + 48, :] = inner[80 * i : 80 * i + 48, px * 128 : px * 128 + 128]
            rs_h[i, 32 * px : 32 * px + 32, :] = inner[
                80 * i + 48 : 80 * i + 80, px * 128 : px * 128 + 128
            ]
    finish_g = direct_sum("g", rs_g, in_g, x, at_x)
    finish_h = direct_sum("h", rs_h, in_h, y, at_y)
    finish_gu = direct_sum("gu", rs_gu, in_gu, x, at_x)

    h_1 = finish_h()
    for px in range(4):
        rs_h2[px] = h_1[px * 32 : px * 32 + 32].astype(BF16)
    finish_h2 = direct_sum("h2", rs_h2, in_h2, x, at_x)
    g_1 = finish_g()
    for py in range(4):
        rs_g2[py] = g_1[py * 48 : py * 48 + 48].astype(BF16)
    finish_g2 = direct_sum("g2", rs_g2, in_g2, y, at_y)
    gd_1 = finish_gd()
    for px in range(4):
        rs_gd2[px] = gd_1[px * 128 : px * 128 + 128].astype(BF16)
    finish_gd2 = direct_sum("gd2", rs_gd2, in_gd2, x, at_x)
    gu_1 = finish_gu()
    lane128 = iota((128, 128), 1)
    for py in range(4):
        first = gu_1[(py % 2) * 256 : (py % 2) * 256 + 128]
        second = gu_1[(py % 2) * 256 + 128 : (py % 2) * 256 + 256]
        if py // 2 == 0:
            pair = jnp.where(lane128 < 64, first, pltpu.roll(second, 64, 1))
        else:
            pair = jnp.where(lane128 < 64, pltpu.roll(first, 64, 1), second)
        rs_gu2[py] = pair.astype(BF16)
    finish_gu2 = direct_sum("gu2", rs_gu2, in_gu2, y, at_y)
    h_2 = finish_h2()
    g_2 = finish_g2()

    zg[0] = g_2.astype(BF16)
    zg[1] = jnp.concatenate([g_2[32:48], h_2], axis=0).astype(BF16)
    inner_copies = []
    for step in range(1, 8):
        to = (z + step) % 8
        copy = describe(
            zg.at[to % 2], zgr.at[step - 1], at_z(step), N_SEND + step - 1, "zg%d" % step
        )
        goes = to // 2 == y
        pl.when(goes)(copy.start)
        inner_copies.append((copy, goes))
    gd_2 = finish_gd2()
    gu_2 = finish_gu2()
    lane32 = iota((32, 128), 1)
    for pz in range(8):
        up = gu_2[(pz % 4) * 32 : (pz % 4) * 32 + 32]
        if pz // 4 == 1:
            up = pltpu.roll(up, 64, 1)
        down = gd_2[(pz // 2) * 32 : (pz // 2) * 32 + 32]
        if pz % 2 == 0:
            down = pltpu.roll(down, 64, 1)
        zs[pz] = jnp.where(lane32 < 64, up, down).astype(BF16)
    last = []
    for step in range(1, 8):
        last.append(send("z%d" % step, zs.at[(z + step) % 8], zr.at[step - 1], at_z(step)))

    spread = []
    for step in range(4):
        for pc in range(2):
            for half in range(2):
                target = device((x + step) % 4, pc, core + 2 * half, z)
                slot = N_SEND + 7 + len(spread)
                copy = describe(ag, gr.at[x], target, slot, "ag%d" % step)
                goes = holder
                if step == 0:
                    goes = holder & ((core != pc) | (y != core + 2 * half))
                spread.append((copy, goes))

    @pl.when(holder)
    def _():
        total = zg[z % 2].astype(F32)
        for step in range(1, 8):
            inner_copies[step - 1][0].wait_recv()
            total = total + zgr[step - 1].astype(F32)
        ag[...] = total.astype(BF16)

    for copy, goes in spread:
        pl.when(goes)(copy.start)

    @pl.when(mine)
    def _():
        gr[x] = ag[...]

    result = zs[z].astype(F32)
    for step in range(1, 8):
        last[step - 1].wait_recv()
        result = result + zr[step - 1].astype(F32)
    sums_ref[0:32, :] = result
    pl.when(jnp.logical_not(mine))(spread[0][0].wait_recv)
    for step in range(1, 4):
        spread[step * 4][0].wait_recv()
    rows_b = jnp.concatenate([gr[i] for i in range(4)], axis=1)
    columns = pl.ds(pl.multiple_of((x * 4 + core * 2 + seg) * 80, 16), 80)
    product = dot_nt(rows_b, wembed[columns, :])
    product = jnp.where(z % 2 == 0, product[0:40], product[8:48])
    sums_ref[32:72, 0:80] = product
    for copy, goes in inner_copies + spread:
        pl.when(goes)(copy.wait_send)
    for copy in started[-N_SEND:]:
        copy.wait_send()


def split_sums(sums_ref, go_ref, gu_ref, gd_ref):
    go_ref[...] = sums_ref[32:72, 0:80]
    gu_ref[...] = sums_ref[0:32, 0:64]
    gd_ref[...] = pltpu.roll(sums_ref[0:32, :], 64, 1)[:, 0:64]


def on_device(
    tokens, targets, visible, w_qkv, w_out, w_embed, mask_token, dec_pos, w_up, w_down, w_head
):
    names.clear()
    anywhere = pl.BlockSpec(memory_space=pl.ANY)
    vmem = pl.BlockSpec(memory_space=pltpu.VMEM)

    def low(*shape):
        return pltpu.VMEM(shape, BF16)

    def wide(*shape):
        return pltpu.VMEM(shape, F32)

    scratch = [
        low(TILE, D), low(PIX, TILE), low(D, INNER), low(D, INNER), low(D, INNER), low(INNER, D),
        low(D, DEC), low(TILE, DEC), low(DEC, FF), low(FF, DEC), low(PIX, DEC),
        low(ROWS, TILE), wide(TILE, 128), low(ROWS, D), low(HEADS, ROWS, 256), low(2, ROWS, 256),
        low(2, PART, 128), low(2, 4, PART, 128), low(2, 4, PART, 128),
        low(2, 16 * ROWS, 128), low(2, 16 * ROWS, 128), low(2, 2 * ROWS, 128),
        wide(2, 2 * ROWS, 128), wide(2, 2 * ROWS, 128),
        low(2, 2, ROWS, 128), low(4, 2, SLOTS, 128), low(2, SLOTS, 320), low(SLOTS, 320),
        wide(SLOTS, DEC), wide(SLOTS, PIX), wide(SLOTS, 128),
        low(HALF, DEC), low(HALF, FF), low(2, HALF, 256), low(2, HALF, DEC),
        low(HALF, DEC), low(HALF, FF), low(HALF, 256), low(HALF, DEC),
        wide(256, FF), wide(DEC, DEC),
        low(SLOTS, DEC), low(SLOTS, FF), low(2, SLOTS, 256), low(2, SLOTS, DEC), low(SLOTS, DEC),
        low(SLOTS, DEC), low(SLOTS, FF), low(SLOTS, 256), low(SLOTS, DEC), low(SLOTS, DEC),
        low(4, 512, 128), low(4, 512, 128), low(4, 192, 128), low(4, 128, 128),
        low(4, 128, 128), low(4, 128, 128), low(4, 48, 128), low(4, 32, 128),
        low(3, 512, 128), low(3, 512, 128), low(3, 192, 128), low(3, 128, 128),
        low(3, 128, 128), low(3, 128, 128), low(3, 48, 128), low(3, 32, 128),
        low(8, 32, 128), low(7, 32, 128), low(2, 48, 128), low(7, 48, 128), low(48, 128),
        low(4, 48, 128),
        pltpu.SemaphoreType.DMA((N_SEND + 7 + 16,)),
        pltpu.SemaphoreType.DMA((N_RECV,)),
        pltpu.SemaphoreType.DMA((N_LOCAL,)),
    ]
    sums = pl.pallas_call(
        kernel,
        out_shape=jax.ShapeDtypeStruct((80, 128), F32),
        in_specs=[
            anywhere, anywhere, vmem, anywhere, anywhere, anywhere, vmem, anywhere, anywhere,
            anywhere, anywhere,
        ],
        out_specs=vmem,
        scratch_shapes=scratch,
        compiler_params=pltpu.CompilerParams(
            collective_id=0, has_side_effects=True, vmem_limit_bytes=56 * 1024 * 1024
        ),
    )(
        tokens[0], targets[0].T, visible, w_qkv, w_out, w_embed, mask_token, dec_pos, w_up,
        w_down, w_head.T,
    )
    grad_out, grad_up, grad_down = pl.pallas_call(
        split_sums,
        out_shape=(
            jax.ShapeDtypeStruct((40, 80), F32),
            jax.ShapeDtypeStruct((32, 64), F32),
            jax.ShapeDtypeStruct((32, 64), F32),
        ),
        in_specs=[vmem],
        out_specs=(vmem, vmem, vmem),
    )(sums)
    return grad_out, grad_up, grad_down.T


def solution(mesh):
    in_specs = (
        P("dp", "blk", None),
        P("dp", "blk", None),
        P("dp", "blk"),
        P(),
        P(),
        P(),
        P(),
        P("blk", None),
        P(),
        P(),
        P(),
    )
    out_specs = (
        P("blk", ("dp", "segment")),
        P("blk", ("dp", "segment")),
        P("blk", ("dp", "segment")),
    )
    return jax.shard_map(
        on_device, mesh=mesh, in_specs=in_specs, out_specs=out_specs, check_vma=False
    )
```

```python
import math

import jax
import jax.numpy as jnp
from jax import lax
from jax.experimental import pallas as pl
from jax.experimental.pallas import tpu as pltpu
from jax.sharding import PartitionSpec as P

MESH = pl.DeviceIdType.MESH
F32 = jnp.float32
BF16 = jnp.bfloat16

HEADS = 8
HEAD_DIM = 80
VIS_TILE = 96
TILE = 384
CAP = 168
ROWS = 176
D = 1280
DEC = 512
FF = 1024
PIX = 1176
INNER = 640
HALF = 192
SLOTS = 96
SEG_STEP = 80
PART = 448
EPS = 1e-05
OUT_MASK = -1e30


def dot(a, b):
    return lax.dot_general(a, b, (((1,), (0,)), ((), ())), preferred_element_type=F32)


def dot_nt(a, b):
    return lax.dot_general(a, b, (((1,), (1,)), ((), ())), preferred_element_type=F32)


def dot_tn(a, b):
    return lax.dot_general(a, b, (((0,), (0,)), ((), ())), preferred_element_type=F32)


def normalize(rows):
    center = rows - jnp.mean(rows, axis=-1, keepdims=True)
    inverse = lax.rsqrt(jnp.mean(center * center, axis=-1, keepdims=True) + EPS)
    return center * inverse, inverse


def iota(shape, axis):
    return lax.broadcasted_iota(jnp.int32, shape, axis)


names = []


def ident(name):
    if name not in names:
        names.append(name)
    return names.index(name)


N_SEND = 32
N_NAMED = 75
N_LOCAL = 14


def kernel(
    tokens_h, targets_h, vis_ref, wqkv_h, wout_h, wembed_h, mtok_ref, dpos_h, wup_h, wdown_h, whead_h,
    sums_ref,
    tokens, targets, wq, wk, wv, wout, wembed, dpos, wup, wdown, whead,
    selector, seen_col, packed, heads, other, kv_own, kv_r, kv_l, keys, vals, qx, acc, top,
    att_out, att_in, att, att_sib, pos_slot, tgt_slot, mask_slot,
    unit_m, act_m, og_m, hg_m, unit_ms, act_ms, og_ms, hg_ms, gd_acc, gu_acc,
    unit_v, act_v, og_v, hg_v, sg_v, unit_vs, act_vs, og_vs, hg_vs, sg_vs,
    rs_gd, rs_gu, rs_g, rs_gd2, rs_gu2,
    in_gd, in_gu, in_g, in_gd2, in_gu2,
    zs, zr, zg, zgr, ag, gr,
    send_sem, recv_sem, load_sem,
):
    dp = lax.axis_index("dp")
    seg = lax.axis_index("segment")
    blk = lax.axis_index("blk")
    x, core = dp // 2, dp % 2
    y, z = seg * 2 + blk // 8, blk % 8
    y_lo = blk // 8

    def device(px, pc, py, pz):
        return (px * 2 + pc, py // 2, (py % 2) * 8 + pz)

    def at_x(step):
        return device((x + step + 4) % 4, core, y, z)

    def at_y(step):
        return device(x, core, (y + step + 4) % 4, z)

    def at_z(step):
        return device(x, core, y, (z + step + 8) % 8)

    sibling = device(x, 1 - core, y, z)

    loads = {}

    def load(name, src, dst):
        copy = pltpu.make_async_copy(src, dst, load_sem.at[len(loads)])
        copy.start()
        loads[name] = copy

    load("tokens", tokens_h, tokens)
    for name, dst, first in (("wk", wk, 640), ("wv", wv, 1280), ("wq", wq, 0)):
        for part in range(2):
            span = pl.ds(part * 640, 640)
            load(name + str(part), wqkv_h.at[span, pl.ds(first, 640)], dst.at[span])

    barrier = pltpu.get_barrier_semaphore()
    user = core == y_lo
    peers = [sibling] + [at_z(step) for step in range(1, 8)]
    peers += [at_x(step) for step in range(1, 4)] + [at_y(step) for step in range(1, 4)]
    for peer in peers:
        pl.semaphore_signal(barrier, inc=1, device_id=peer, device_id_type=MESH)
    for px in range(4):
        for py in range(4):
            source = device((x + px) % 4, y_lo, (y + py) % 4, z)

            def greet():
                pl.semaphore_signal(barrier, inc=1, device_id=source, device_id_type=MESH)

            if px or py:
                greet()
            else:
                pl.when(jnp.logical_not(user))(greet)
    greetings = len(peers) + 16 - jnp.where(user, 1, 0)

    started = []

    def describe(src, dst, target, slot, name):
        return pltpu.make_async_remote_copy(
            src_ref=src,
            dst_ref=dst,
            send_sem=send_sem.at[slot],
            recv_sem=recv_sem.at[ident(name) if isinstance(name, str) else name],
            device_id=target,
            device_id_type=MESH,
        )

    def send(name, src, dst, target):
        count = len(started)
        if count >= N_SEND:
            started[count - N_SEND].wait_send()
        copy = describe(src, dst, target, count % N_SEND, name)
        copy.start()
        started.append(copy)
        return copy

    vis = vis_ref[...].astype(F32)
    tri = (iota((TILE, TILE), 0) <= iota((TILE, TILE), 1)).astype(F32).astype(BF16)
    vis8 = jnp.broadcast_to(vis, (8, TILE))
    position = dot(vis8.astype(BF16), tri)[0:1, :] - 1.0
    count = jnp.sum(vis, axis=1, keepdims=True)
    slot_ids = iota((ROWS, TILE), 0).astype(F32)
    chosen = jnp.where((position == slot_ids) & (vis > 0.5), 1.0, 0.0).astype(BF16)
    selector[...] = chosen
    loads["tokens"].wait()
    rows = dot(chosen, tokens[...])
    packed[...] = rows.astype(BF16)
    normed = normalize(rows)[0].astype(BF16)
    seen_col[...] = dot_tn(chosen, jnp.ones((ROWS, 128), BF16))
    projected = []
    for name, weight in (("wk", wk), ("wv", wv), ("wq", wq)):
        loads[name + "0"].wait()
        loads[name + "1"].wait()
        projected.append(dot(normed, weight[...]))
    load("dpos", dpos_h, dpos)
    load("targets", targets_h, targets)
    load("wup", wup_h, wup)
    load("wdown", wdown_h, wdown)
    load("whead", whead_h, whead)
    load("wout", wout_h, wout)
    load("wembed", wembed_h, wembed)
    slot_row = iota((ROWS, 256), 0)
    for h in range(HEADS):
        parts = [p[:, h * 80 : h * 80 + 80] for p in projected]
        block = jnp.concatenate(parts + [jnp.zeros((ROWS, 16), F32)], axis=1)
        block = jnp.where(slot_row >= CAP, count, block)
        heads[h] = block.astype(BF16)

    pl.semaphore_wait(barrier, greetings)
    up_head = ((y + 1) % 4) * 2
    down_head = ((y + 3) % 4) * 2 + 1
    from_down = send("qkv+", heads.at[up_head], other.at[0], at_y(1))
    from_up = send("qkv-", heads.at[down_head], other.at[1], at_y(-1))

    lane = iota((ROWS, 128), 1)
    slot128 = iota((ROWS, 128), 0).astype(F32)

    def make_query(block, j, first):
        window = pltpu.roll(block[:, 128:256].astype(F32), 96, 1)
        query = jnp.where(lane < 80, window, jnp.where(lane == 80, 1.0, 0.0))
        qx[j, first : first + ROWS, :] = query.astype(BF16)

    lane88 = iota((ROWS // 2, 128), 1)

    def fold(first, second, part):
        both = jnp.concatenate(
            [first[:, 0:160].astype(F32), second[:, 0:160].astype(F32), jnp.zeros((ROWS, 64), F32)],
            axis=1,
        )
        third = both[:, 256:384]
        third = jnp.where(lane88 < 64, third[0:88], pltpu.roll(third[88:ROWS], 64, 1))
        part[0:ROWS, :] = both[:, 0:128].astype(BF16)
        part[ROWS : 2 * ROWS, :] = both[:, 128:256].astype(BF16)
        third = jnp.concatenate([third, jnp.zeros((8, 128), F32)], axis=0)
        part[2 * ROWS : PART, :] = third.astype(BF16)

    def unfold(part, first):
        p0 = part[0:ROWS, :].astype(F32)
        p1 = part[ROWS : 2 * ROWS, :].astype(F32)
        third = part[2 * ROWS : PART, :].astype(F32)[0:88]
        p2 = jnp.concatenate([third, pltpu.roll(third, 64, 1)], axis=0)
        pairs = (
            (p0, pltpu.roll(jnp.concatenate([p0, p1], axis=1), 176, 1)),
            (pltpu.roll(p1, 96, 1), pltpu.roll(jnp.concatenate([p1, p2], axis=1), 144, 1)),
        )
        for j in range(2):
            key, value = pairs[j]
            counts = key[CAP : CAP + 1, :]
            outside = jnp.where((lane == 80) & (slot128 >= counts), OUT_MASK, 0.0)
            keys[j, first : first + ROWS, :] = jnp.where(lane < 80, key, outside).astype(BF16)
            vals[j, first : first + ROWS, :] = jnp.where(
                lane == 80, 1.0, value[:, 0:128]
            ).astype(BF16)

    ring = {}
    ring_halves = (pl.ds(0, PART // 2), pl.ds(PART // 2, PART // 2))

    def ring_send(way, part, step, half, src):
        buffer, to = (kv_r, 1) if way == "r" else (kv_l, -1)
        rows_of = ring_halves[half]
        ring[way, part, step, half] = send(
            "%s%d%d%d" % (way, step, part, half),
            src.at[rows_of],
            buffer.at[part, step, rows_of],
            at_z(to),
        )

    def ring_start(part):
        for half in range(2):
            for way in "rl":
                ring_send(way, part, 0, half, kv_own.at[part])

    def ring_next(part, step):
        for half in range(2):
            for way, buffer in (("r", kv_r), ("l", kv_l)):
                ring[way, part, step, half].wait_recv()
                if step < 2 or (step == 2 and (way == "r") == (part == 0)):
                    ring_send(way, part, step + 1, half, buffer.at[part, step])

    own = [heads[y * 2], heads[y * 2 + 1]]
    fold(own[0], own[1], kv_own.at[0])
    ring_start(0)
    for j in range(2):
        make_query(own[j], j, 0)
    from_down.wait_recv()
    from_up.wait_recv()
    others = [other[0], other[1]]
    fold(others[0], others[1], kv_own.at[1])
    ring_start(1)
    for j in range(2):
        make_query(others[j], j, ROWS)

    scale = math.log2(math.e) / math.sqrt(HEAD_DIM)

    def attend_head(j, first, begin=False):
        span = slice(first, first + 2 * ROWS)
        scores = dot_nt(qx[j], keys[j, span, :])
        best = jnp.max(scores, axis=1, keepdims=True)
        if not begin:
            before = top[j]
            best = jnp.maximum(before[:, 0:1], best)
        probs = jnp.exp2((scores - best) * scale).astype(BF16)
        term = dot(probs, vals[j, span, :])
        if not begin:
            term = term + acc[j] * jnp.exp2((before - best) * scale)
        acc[j] = term
        top[j] = jnp.broadcast_to(best, (2 * ROWS, 128))

    def attend(first, one, two, begin=False):
        unfold(one, first)
        unfold(two, first + ROWS)
        for j in range(2):
            attend_head(j, first, begin)

    grad_scale = 8.0 / math.sqrt(8 * 16 * (TILE - VIS_TILE))
    root_half = 1.0 / math.sqrt(2.0)
    order = iota((DEC, DEC), 1)
    source = (order // 32 % 4) * 128 + (order // 256) * 64 + (order // 128 % 2) * 32 + order % 32
    shuffle = (iota((DEC, DEC), 0) == source).astype(F32).astype(BF16)

    def decode_forward(stream, goal, keep, unit, act, ready):
        normal, inverse = normalize(stream)
        low = normal.astype(BF16)
        unit[...] = low
        hidden = dot(low, wup[...])
        cumulative = 0.5 * (1.0 + lax.erf(hidden * root_half))
        active = (hidden * cumulative).astype(BF16)
        act[...] = active
        ready()
        slope = cumulative + hidden * jnp.exp(-0.5 * hidden * hidden) * (
            1.0 / math.sqrt(2.0 * math.pi)
        )
        stream_out = stream + dot(active, wdown[...])
        predicted = dot_nt(stream_out.astype(BF16), whead[...])
        pred_grad = ((predicted - goal) * (keep * grad_scale)).astype(BF16)
        out_grad = dot(pred_grad, whead[...])
        return normal, inverse, slope, out_grad

    def decode_hidden(out_low, slope, hg):
        hidden_grad = (dot_nt(out_low, wdown[...]) * slope).astype(BF16)
        for c in range(2):
            for px in range(4):
                at = px * 256 + c * 128
                hg[c, :, px * 128 : px * 128 + 128] = hidden_grad[:, at : at + 128]
        return hidden_grad

    def split_out(out_low, og):
        mixed = dot(out_low, shuffle).astype(BF16)
        og[0] = mixed[:, 0:256]
        og[1] = mixed[:, 256:512]

    attend(0, kv_own.at[0], kv_own.at[1], begin=True)
    for name in ("dpos", "targets", "wup", "wdown", "whead"):
        loads[name].wait()
    ring_next(0, 0)
    part_rows = pl.ds(pl.multiple_of(seg * HALF, 16), HALF)
    stream_m = mtok_ref[...].astype(F32)[None, :] + dpos[part_rows, :].astype(F32)
    patch = iota((HALF, TILE), 0) + seg * HALF
    pick = (iota((HALF, TILE), 1) == patch).astype(F32).astype(BF16)
    goal_m = dot_nt(pick, targets[...])
    keep_m = 1.0 - seen_col[part_rows, :][:, 0:1]
    masked = []

    def ready_m():
        masked.append(send("unit_m", unit_m, unit_ms, sibling))
        masked.append(send("act_m", act_m, act_ms, sibling))
        ring_next(1, 0)

    normal, inverse, slope, out_grad = decode_forward(
        stream_m, goal_m, keep_m, unit_m, act_m, ready_m
    )
    attend(2 * ROWS, kv_r.at[0, 0], kv_l.at[0, 0])
    ring_next(0, 1)
    out_low = out_grad.astype(BF16)
    split_out(out_low, og_m)
    masked.append(send("og_m", og_m.at[1 - core], og_ms, sibling))
    decode_hidden(out_low, slope, hg_m)
    masked.append(send("hg_m", hg_m.at[1 - core], hg_ms, sibling))
    attend(4 * ROWS, kv_r.at[1, 0], kv_l.at[1, 0])
    ring_next(1, 1)
    attend(6 * ROWS, kv_r.at[0, 1], kv_l.at[0, 1])
    slot_first = pl.multiple_of(seg * SEG_STEP, 16)
    slot_rows = pl.ds(slot_first, SLOTS)
    chosen_part = selector[slot_rows, :]
    pos_slot[...] = dot(chosen_part, dpos[...])
    tgt_slot[...] = dot_nt(chosen_part, targets[...])
    number = iota((SLOTS, 128), 0) + seg * SEG_STEP
    kept = (number.astype(F32) < count) & (number >= seg * SLOTS)
    mask_slot[...] = jnp.where(kept, 1.0, 0.0)
    ring_next(0, 2)
    attend(8 * ROWS, kv_r.at[1, 1], kv_l.at[1, 1])
    for copy in masked:
        copy.wait_recv()
    gd_acc[...] = dot_tn(og_m[core], act_m[...]) + dot_tn(og_ms[...], act_ms[...])
    ring_next(1, 2)
    attend(10 * ROWS, kv_r.at[0, 2], kv_l.at[0, 2])
    gu_acc[...] = dot_tn(unit_m[...], hg_m[core]) + dot_tn(unit_ms[...], hg_ms[...])
    attend(12 * ROWS, kv_r.at[1, 2], kv_l.at[1, 2])
    loads["wout"].wait()
    loads["wembed"].wait()
    for half in range(2):
        ring["r", 0, 3, half].wait_recv()
        ring["l", 1, 3, half].wait_recv()
    unfold(kv_r.at[0, 3], 14 * ROWS)
    unfold(kv_l.at[1, 3], 15 * ROWS)

    back = []
    for j in range(2):
        attend_head(j, 14 * ROWS)
        total = acc[j]
        done = (total * (1.0 / total[:, 80:81])).astype(BF16)
        att_out[j, 0] = done[0:ROWS]
        att_out[j, 1] = done[ROWS : 2 * ROWS]
        for step, i in ((2, 0), (1, 1), (-1, 1)):
            goal_seg = ((y + step + 4) % 4) // 2
            span = pl.ds(pl.multiple_of(goal_seg * SEG_STEP, 16), SLOTS)
            back.append(
                send("b%d%d" % (j, step + 4), att_out.at[j, i, span], att_in.at[y, j], at_y(step))
            )
        att_in[y, j] = att_out[j, 0, slot_rows, :]
    for copy in back:
        copy.wait_recv()
    pieces = [att_in[i // 2, i % 2][:, 0:80].astype(F32) for i in range(HEADS)]
    for c in range(2):
        att[c] = jnp.concatenate(pieces[c * 4 : c * 4 + 4], axis=1).astype(BF16)
    swap_att = send("att_s", att.at[1 - core], att_sib, sibling)
    attended = jnp.concatenate(pieces, axis=1).astype(BF16)

    encoded = packed[slot_rows, :].astype(F32) + dot(attended, wout[...])
    embedded = dot(encoded.astype(BF16), wembed[...])
    stream_v = embedded + pos_slot[...]
    swap = {}

    def ready_v():
        swap["unit"] = send("unit_v", unit_v, unit_vs, sibling)
        swap["act"] = send("act_v", act_v, act_vs, sibling)

    normal, inverse, slope, out_grad = decode_forward(
        stream_v, tgt_slot[...], mask_slot[:, 0:1], unit_v, act_v, ready_v
    )
    out_low = out_grad.astype(BF16)
    split_out(out_low, og_v)
    swap["og"] = send("og_v", og_v.at[1 - core], og_vs, sibling)
    hidden_grad = decode_hidden(out_low, slope, hg_v)
    swap["hg"] = send("hg_v", hg_v.at[1 - core], hg_vs, sibling)

    def direct_sum(name, chunks, landing, place, at):
        copies = [
            send(name + str(step), chunks.at[(place + step) % 4], landing.at[step - 1], at(step))
            for step in range(1, 4)
        ]

        def finish():
            total = chunks[place].astype(F32)
            for step in range(3):
                copies[step].wait_recv()
                total = total + landing[step].astype(F32)
            return total

        return finish

    swap["act"].wait_recv()
    swap["og"].wait_recv()
    gd_t = gd_acc[...] + dot_tn(og_v[core], act_v[...]) + dot_tn(og_vs[...], act_vs[...])
    gd_t = gd_t.astype(BF16)
    for py in range(4):
        for px in range(4):
            for k in range(4):
                r = (py // 2) * 128 + px * 32
                c = (py % 2) * 512 + k * 128
                at = px * 128 + k * 32
                rs_gd[py, at : at + 32, :] = gd_t[r : r + 32, c : c + 128]
    finish_gd = direct_sum("gd", rs_gd, in_gd, y, at_y)

    unit_grad = dot_nt(hidden_grad, wup[...])
    cross = jnp.mean(unit_grad * normal, axis=-1, keepdims=True)
    middle = jnp.mean(unit_grad, axis=-1, keepdims=True)
    stream_grad = out_grad + inverse * (unit_grad - middle - normal * cross)
    sg_v[...] = stream_grad.astype(BF16)
    swap["sg"] = send("sg_v", sg_v, sg_vs, sibling)

    swap["unit"].wait_recv()
    swap["hg"].wait_recv()
    gu_t = gu_acc[...] + dot_tn(unit_v[...], hg_v[core]) + dot_tn(unit_vs[...], hg_vs[...])
    gu_t = gu_t.astype(BF16)
    for px in range(4):
        rs_gu[px] = gu_t[:, px * 128 : px * 128 + 128]

    swap_att.wait_recv()
    swap["sg"].wait_recv()
    inner = dot_tn(att[core], sg_v[...]) + dot_tn(att_sib[...], sg_vs[...])
    inner = inner.astype(BF16)
    for py in range(4):
        rs_g[py] = inner[:, py * 128 : py * 128 + 128]
    finish_g = direct_sum("g", rs_g, in_g, y, at_y)
    finish_gu = direct_sum("gu", rs_gu, in_gu, x, at_x)

    g_1 = finish_g()
    for pz in range(8):
        piece = jnp.concatenate([g_1[40 * pz : 40 * pz + 40], jnp.zeros((8, 128), F32)], axis=0)
        zg[pz] = piece.astype(BF16)
    row_copies = [
        send("zg%d" % step, zg.at[(z + step) % 8], zgr.at[step - 1], at_z(step))
        for step in range(1, 8)
    ]
    gd_1 = finish_gd()
    for px in range(4):
        rs_gd2[px] = gd_1[px * 128 : px * 128 + 128].astype(BF16)
    finish_gd2 = direct_sum("gd2", rs_gd2, in_gd2, x, at_x)
    gu_1 = finish_gu()
    lane128 = iota((128, 128), 1)
    for py in range(4):
        first = gu_1[(py % 2) * 256 : (py % 2) * 256 + 128]
        second = gu_1[(py % 2) * 256 + 128 : (py % 2) * 256 + 256]
        if py // 2 == 0:
            pair = jnp.where(lane128 < 64, first, pltpu.roll(second, 64, 1))
        else:
            pair = jnp.where(lane128 < 64, pltpu.roll(first, 64, 1), second)
        rs_gu2[py] = pair.astype(BF16)
    finish_gu2 = direct_sum("gu2", rs_gu2, in_gu2, y, at_y)
    total = zg[z].astype(F32)
    for step in range(1, 8):
        row_copies[step - 1].wait_recv()
        total = total + zgr[step - 1].astype(F32)
    ag[...] = total.astype(BF16)
    spread = []
    for px in range(4):
        for pc in range(2):
            for half in range(2):
                target = device((x + px) % 4, pc, core + 2 * half, z)
                away = None
                if px == 0:
                    away = (core != pc) | (y != core + 2 * half)
                slot = N_SEND + len(spread)
                copy = describe(ag, gr.at[y, x], target, slot, N_NAMED + y * 4 + x)
                if away is None:
                    copy.start()
                else:
                    pl.when(away)(copy.start)
                spread.append((copy, away))

    @pl.when(user)
    def _():
        gr[y, x] = ag[...]

    gd_2 = finish_gd2()
    gu_2 = finish_gu2()
    lane32 = iota((32, 128), 1)
    for pz in range(8):
        up = gu_2[(pz % 4) * 32 : (pz % 4) * 32 + 32]
        if pz // 4 == 1:
            up = pltpu.roll(up, 64, 1)
        down = gd_2[(pz // 2) * 32 : (pz // 2) * 32 + 32]
        if pz % 2 == 0:
            down = pltpu.roll(down, 64, 1)
        zs[pz] = jnp.where(lane32 < 64, up, down).astype(BF16)
    last = []
    for step in range(1, 8):
        last.append(send("z%d" % step, zs.at[(z + step) % 8], zr.at[step - 1], at_z(step)))

    result = zs[z].astype(F32)
    for step in range(1, 8):
        last[step - 1].wait_recv()
        result = result + zr[step - 1].astype(F32)
    sums_ref[0:32, :] = result
    for py in range(4):
        for px in range(4):
            landed = describe(ag, gr.at[py, px], sibling, 0, N_NAMED + py * 4 + px)
            here = user & (y == py) & (x == px)
            pl.when(jnp.logical_not(here))(landed.wait_recv)
    rows_b = []
    for py in range(4):
        total = gr[py, 0].astype(F32)
        for px in range(1, 4):
            total = total + gr[py, px].astype(F32)
        rows_b.append(total.astype(BF16))
    rows_b = jnp.concatenate(rows_b, axis=1)
    columns = pl.ds(pl.multiple_of((x * 4 + core * 2 + seg) * 80, 16), 80)
    sums_ref[32:72, 0:80] = dot_nt(rows_b, wembed[columns, :])[0:40]
    for copy, away in spread:
        if away is None:
            copy.wait_send()
        else:
            pl.when(away)(copy.wait_send)
    for copy in started[-N_SEND:]:
        copy.wait_send()


def split_sums(sums_ref, go_ref, gu_ref, gd_ref):
    go_ref[...] = sums_ref[32:72, 0:80]
    gu_ref[...] = sums_ref[0:32, 0:64]
    gd_ref[...] = pltpu.roll(sums_ref[0:32, :], 64, 1)[:, 0:64]


def on_device(
    tokens, targets, visible, w_qkv, w_out, w_embed, mask_token, dec_pos, w_up, w_down, w_head
):
    names.clear()
    anywhere = pl.BlockSpec(memory_space=pl.ANY)
    vmem = pl.BlockSpec(memory_space=pltpu.VMEM)

    def low(*shape):
        return pltpu.VMEM(shape, BF16)

    def wide(*shape):
        return pltpu.VMEM(shape, F32)

    scratch = [
        low(TILE, D), low(PIX, TILE), low(D, INNER), low(D, INNER), low(D, INNER), low(INNER, D),
        low(D, DEC), low(TILE, DEC), low(DEC, FF), low(FF, DEC), low(PIX, DEC),
        low(ROWS, TILE), wide(TILE, 128), low(ROWS, D), low(HEADS, ROWS, 256), low(2, ROWS, 256),
        low(2, PART, 128), low(2, 4, PART, 128), low(2, 4, PART, 128),
        low(2, 16 * ROWS, 128), low(2, 16 * ROWS, 128), low(2, 2 * ROWS, 128),
        wide(2, 2 * ROWS, 128), wide(2, 2 * ROWS, 128),
        low(2, 2, ROWS, 128), low(4, 2, SLOTS, 128), low(2, SLOTS, 320), low(SLOTS, 320),
        wide(SLOTS, DEC), wide(SLOTS, PIX), wide(SLOTS, 128),
        low(HALF, DEC), low(HALF, FF), low(2, HALF, 256), low(2, HALF, DEC),
        low(HALF, DEC), low(HALF, FF), low(HALF, 256), low(HALF, DEC),
        wide(256, FF), wide(DEC, DEC),
        low(SLOTS, DEC), low(SLOTS, FF), low(2, SLOTS, 256), low(2, SLOTS, DEC), low(SLOTS, DEC),
        low(SLOTS, DEC), low(SLOTS, FF), low(SLOTS, 256), low(SLOTS, DEC), low(SLOTS, DEC),
        low(4, 512, 128), low(4, 512, 128), low(4, 320, 128), low(4, 128, 128), low(4, 128, 128),
        low(3, 512, 128), low(3, 512, 128), low(3, 320, 128), low(3, 128, 128), low(3, 128, 128),
        low(8, 32, 128), low(7, 32, 128), low(8, 48, 128), low(7, 48, 128), low(48, 128),
        low(4, 4, 48, 128),
        pltpu.SemaphoreType.DMA((N_SEND + 16,)),
        pltpu.SemaphoreType.DMA((N_NAMED + 16,)),
        pltpu.SemaphoreType.DMA((N_LOCAL,)),
    ]
    sums = pl.pallas_call(
        kernel,
        out_shape=jax.ShapeDtypeStruct((80, 128), F32),
        in_specs=[
            anywhere, anywhere, vmem, anywhere, anywhere, anywhere, vmem, anywhere, anywhere,
            anywhere, anywhere,
        ],
        out_specs=vmem,
        scratch_shapes=scratch,
        compiler_params=pltpu.CompilerParams(
            collective_id=0, has_side_effects=True, vmem_limit_bytes=56 * 1024 * 1024
        ),
    )(
        tokens[0], targets[0].T, visible, w_qkv, w_out, w_embed, mask_token, dec_pos, w_up,
        w_down, w_head.T,
    )
    grad_out, grad_up, grad_down = pl.pallas_call(
        split_sums,
        out_shape=(
            jax.ShapeDtypeStruct((40, 80), F32),
            jax.ShapeDtypeStruct((32, 64), F32),
            jax.ShapeDtypeStruct((32, 64), F32),
        ),
        in_specs=[vmem],
        out_specs=(vmem, vmem, vmem),
    )(sums)
    return grad_out, grad_up, grad_down.T


def solution(mesh):
    in_specs = (
        P("dp", "blk", None),
        P("dp", "blk", None),
        P("dp", "blk"),
        P(),
        P(),
        P(),
        P(),
        P("blk", None),
        P(),
        P(),
        P(),
    )
    out_specs = (
        P("blk", ("dp", "segment")),
        P("blk", ("dp", "segment")),
        P("blk", ("dp", "segment")),
    )
    return jax.shard_map(
        on_device, mesh=mesh, in_specs=in_specs, out_specs=out_specs, check_vma=False
    )
```

```python
import math

import jax
import jax.numpy as jnp
from jax import lax
from jax.experimental import pallas as pl
from jax.experimental.pallas import tpu as pltpu
from jax.sharding import PartitionSpec as P

MESH = pl.DeviceIdType.MESH
F32 = jnp.float32
BF16 = jnp.bfloat16

HEADS = 8
HEAD_DIM = 80
VIS_TILE = 96
TILE = 384
CAP = 168
ROWS = 176
D = 1280
DEC = 512
FF = 1024
PIX = 1176
INNER = 640
HALF = 192
SLOTS = 96
SEG_STEP = 80
PART = 448
EPS = 1e-05
OUT_MASK = -1e30


def dot(a, b):
    return lax.dot_general(a, b, (((1,), (0,)), ((), ())), preferred_element_type=F32)


def dot_nt(a, b):
    return lax.dot_general(a, b, (((1,), (1,)), ((), ())), preferred_element_type=F32)


def dot_tn(a, b):
    return lax.dot_general(a, b, (((0,), (0,)), ((), ())), preferred_element_type=F32)


def normalize(rows):
    center = rows - jnp.mean(rows, axis=-1, keepdims=True)
    inverse = lax.rsqrt(jnp.mean(center * center, axis=-1, keepdims=True) + EPS)
    return center * inverse, inverse


def iota(shape, axis):
    return lax.broadcasted_iota(jnp.int32, shape, axis)


names = []


def ident(name):
    if name not in names:
        names.append(name)
    return names.index(name)


N_SEND = 16
N_NAMED = 78
N_LOCAL = 11


def kernel(
    tokens_h, targets_h, vis_ref, wqkv_h, wout_h, wembed_h, mtok_ref, dpos_h, wup_h, wdown_h, whead_h,
    sums_ref,
    tokens, targets, wq, wk, wv, wout, wembed, dpos, wup, wdown, whead,
    selector, seen_col, packed, heads, other, kv_own, kv_r, kv_l, kv_d, keys, vals, qx, acc, top,
    att_out, att_in, att, att_sib, pos_slot, tgt_slot, mask_slot,
    unit_m, act_m, og_m, hg_m, unit_ms, act_ms, og_ms, hg_ms, gd_acc, gu_acc,
    unit_v, act_v, og_v, hg_v, sg_v, unit_vs, act_vs, og_vs, hg_vs, sg_vs,
    rs_gd, rs_gu, rs_g, rs_h, rs_gd2, rs_gu2,
    in_gd, in_gu, in_g, in_h, in_gd2, in_gu2,
    zs, zr, zg, zgr, ag, gr,
    send_sem, recv_sem, load_sem,
):
    dp = lax.axis_index("dp")
    seg = lax.axis_index("segment")
    blk = lax.axis_index("blk")
    x, core = dp // 2, dp % 2
    y, z = seg * 2 + blk // 8, blk % 8
    y_lo = blk // 8

    def device(px, pc, py, pz):
        return (px * 2 + pc, py // 2, (py % 2) * 8 + pz)

    def at_x(step):
        return device((x + step + 4) % 4, core, y, z)

    def at_y(step):
        return device(x, core, (y + step + 4) % 4, z)

    def at_z(step):
        return device(x, core, y, (z + step + 8) % 8)

    sibling = device(x, 1 - core, y, z)

    loads = {}

    def load(name, src, dst):
        copy = pltpu.make_async_copy(src, dst, load_sem.at[len(loads)])
        copy.start()
        loads[name] = copy

    load("tokens", tokens_h, tokens)
    for name, dst, first in (("wk", wk, 640), ("wv", wv, 1280), ("wq", wq, 0)):
        load(name, wqkv_h.at[:, pl.ds(first, 640)], dst)

    barrier = pltpu.get_barrier_semaphore()
    user = core == y_lo
    peers = [sibling] + [at_z(step) for step in range(1, 8)]
    peers += [at_x(step) for step in range(1, 4)] + [at_y(step) for step in range(1, 4)]
    for peer in peers:
        pl.semaphore_signal(barrier, inc=1, device_id=peer, device_id_type=MESH)
    for px in range(4):
        for py in range(4):
            source = device((x + px) % 4, y_lo, (y + py) % 4, z)

            def greet():
                pl.semaphore_signal(barrier, inc=1, device_id=source, device_id_type=MESH)

            if px or py:
                greet()
            else:
                pl.when(jnp.logical_not(user))(greet)
    greetings = len(peers) + 16 - jnp.where(user, 1, 0)

    started = []

    def describe(src, dst, target, slot, name):
        return pltpu.make_async_remote_copy(
            src_ref=src,
            dst_ref=dst,
            send_sem=send_sem.at[slot],
            recv_sem=recv_sem.at[ident(name) if isinstance(name, str) else name],
            device_id=target,
            device_id_type=MESH,
        )

    def send(name, src, dst, target):
        count = len(started)
        if count >= N_SEND:
            started[count - N_SEND].wait_send()
        copy = describe(src, dst, target, count % N_SEND, name)
        copy.start()
        started.append(copy)
        return copy

    vis = vis_ref[...].astype(F32)
    tri = (iota((TILE, TILE), 0) <= iota((TILE, TILE), 1)).astype(F32).astype(BF16)
    vis8 = jnp.broadcast_to(vis, (8, TILE))
    position = dot(vis8.astype(BF16), tri)[0:1, :] - 1.0
    count = jnp.sum(vis, axis=1, keepdims=True)
    slot_ids = iota((ROWS, TILE), 0).astype(F32)
    chosen = jnp.where((position == slot_ids) & (vis > 0.5), 1.0, 0.0).astype(BF16)
    selector[...] = chosen
    loads["tokens"].wait()
    rows = dot(chosen, tokens[...])
    packed[...] = rows.astype(BF16)
    normed = normalize(rows)[0].astype(BF16)
    seen_col[...] = dot_tn(chosen, jnp.ones((ROWS, 128), BF16))
    projected = []
    for name, weight in (("wk", wk), ("wv", wv), ("wq", wq)):
        loads[name].wait()
        projected.append(dot(normed, weight[...]))
    slot_row = iota((ROWS, 256), 0)
    for h in range(HEADS):
        parts = [p[:, h * 80 : h * 80 + 80] for p in projected]
        block = jnp.concatenate(parts + [jnp.zeros((ROWS, 16), F32)], axis=1)
        block = jnp.where(slot_row >= CAP, count, block)
        heads[h] = block.astype(BF16)

    pl.semaphore_wait(barrier, greetings)
    up_head = ((y + 1) % 4) * 2
    down_head = ((y + 3) % 4) * 2 + 1
    from_down = send("qkv+", heads.at[up_head], other.at[0], at_y(1))
    from_up = send("qkv-", heads.at[down_head], other.at[1], at_y(-1))

    lane = iota((ROWS, 128), 1)
    slot128 = iota((ROWS, 128), 0).astype(F32)

    def make_query(block, j, first):
        window = pltpu.roll(block[:, 128:256].astype(F32), 96, 1)
        query = jnp.where(lane < 80, window, jnp.where(lane == 80, 1.0, 0.0))
        qx[j, first : first + ROWS, :] = query.astype(BF16)

    lane88 = iota((ROWS // 2, 128), 1)

    def fold(first, second, part):
        both = jnp.concatenate(
            [first[:, 0:160].astype(F32), second[:, 0:160].astype(F32), jnp.zeros((ROWS, 64), F32)],
            axis=1,
        )
        third = both[:, 256:384]
        third = jnp.where(lane88 < 64, third[0:88], pltpu.roll(third[88:ROWS], 64, 1))
        part[0:ROWS, :] = both[:, 0:128].astype(BF16)
        part[ROWS : 2 * ROWS, :] = both[:, 128:256].astype(BF16)
        third = jnp.concatenate([third, jnp.zeros((8, 128), F32)], axis=0)
        part[2 * ROWS : PART, :] = third.astype(BF16)

    def unfold(part, first):
        p0 = part[0:ROWS, :].astype(F32)
        p1 = part[ROWS : 2 * ROWS, :].astype(F32)
        third = part[2 * ROWS : PART, :].astype(F32)[0:88]
        p2 = jnp.concatenate([third, pltpu.roll(third, 64, 1)], axis=0)
        pairs = (
            (p0, pltpu.roll(jnp.concatenate([p0, p1], axis=1), 176, 1)),
            (pltpu.roll(p1, 96, 1), pltpu.roll(jnp.concatenate([p1, p2], axis=1), 144, 1)),
        )
        for j in range(2):
            key, value = pairs[j]
            counts = key[CAP : CAP + 1, :]
            outside = jnp.where((lane == 80) & (slot128 >= counts), OUT_MASK, 0.0)
            keys[j, first : first + ROWS, :] = jnp.where(lane < 80, key, outside).astype(BF16)
            vals[j, first : first + ROWS, :] = jnp.where(
                lane == 80, 1.0, value[:, 0:128]
            ).astype(BF16)

    ring = {}
    ring_halves = (pl.ds(0, PART // 2), pl.ds(PART // 2, PART // 2))

    def ring_send(way, part, step, half, src):
        buffer, to = (kv_r, 1) if way == "r" else (kv_l, -1)
        rows_of = ring_halves[half]
        ring[way, part, step, half] = send(
            "%s%d%d%d" % (way, step, part, half),
            src.at[rows_of],
            (buffer if step < 3 else kv_d).at[part, step % 3, rows_of],
            at_z(to),
        )

    def ring_start(part):
        for half in range(2):
            for way in "rl":
                ring_send(way, part, 0, half, kv_own.at[part])

    def ring_next(part, step):
        for half in range(2):
            for way, buffer in (("r", kv_r), ("l", kv_l)):
                ring[way, part, step, half].wait_recv()
                if step < 2 or (way == "r") == (half == 0):
                    ring_send(way, part, step + 1, half, buffer.at[part, step])

    own = [heads[y * 2], heads[y * 2 + 1]]
    fold(own[0], own[1], kv_own.at[0])
    ring_start(0)
    load("dpos", dpos_h, dpos)
    load("targets", targets_h, targets)
    load("wup", wup_h, wup)
    load("wdown", wdown_h, wdown)
    load("whead", whead_h, whead)
    load("wout", wout_h, wout)
    load("wembed", wembed_h, wembed)
    for j in range(2):
        make_query(own[j], j, 0)
    from_down.wait_recv()
    from_up.wait_recv()
    others = [other[0], other[1]]
    fold(others[0], others[1], kv_own.at[1])
    ring_start(1)
    for j in range(2):
        make_query(others[j], j, ROWS)

    scale = math.log2(math.e) / math.sqrt(HEAD_DIM)

    def attend_head(j, first, begin=False):
        span = slice(first, first + 2 * ROWS)
        scores = dot_nt(qx[j], keys[j, span, :])
        best = jnp.max(scores, axis=1, keepdims=True)
        if not begin:
            before = top[j]
            best = jnp.maximum(before[:, 0:1], best)
        probs = jnp.exp2((scores - best) * scale).astype(BF16)
        term = dot(probs, vals[j, span, :])
        if not begin:
            term = term + acc[j] * jnp.exp2((before - best) * scale)
        acc[j] = term
        top[j] = jnp.broadcast_to(best, (2 * ROWS, 128))

    def attend(first, one, two, begin=False):
        unfold(one, first)
        unfold(two, first + ROWS)
        for j in range(2):
            attend_head(j, first, begin)

    grad_scale = 8.0 / math.sqrt(8 * 16 * (TILE - VIS_TILE))
    root_half = 1.0 / math.sqrt(2.0)
    order = iota((DEC, DEC), 1)
    source = (order // 32 % 4) * 128 + (order // 256) * 64 + (order // 128 % 2) * 32 + order % 32
    shuffle = (iota((DEC, DEC), 0) == source).astype(F32).astype(BF16)

    def decode_forward(stream, goal, keep, unit, act, ready):
        normal, inverse = normalize(stream)
        low = normal.astype(BF16)
        unit[...] = low
        hidden = dot(low, wup[...])
        cumulative = 0.5 * (1.0 + lax.erf(hidden * root_half))
        active = (hidden * cumulative).astype(BF16)
        act[...] = active
        ready()
        slope = cumulative + hidden * jnp.exp(-0.5 * hidden * hidden) * (
            1.0 / math.sqrt(2.0 * math.pi)
        )
        stream_out = stream + dot(active, wdown[...])
        predicted = dot_nt(stream_out.astype(BF16), whead[...])
        pred_grad = ((predicted - goal) * (keep * grad_scale)).astype(BF16)
        out_grad = dot(pred_grad, whead[...])
        return normal, inverse, slope, out_grad

    def decode_hidden(out_low, slope, hg):
        hidden_grad = (dot_nt(out_low, wdown[...]) * slope).astype(BF16)
        for c in range(2):
            for px in range(4):
                at = px * 256 + c * 128
                hg[c, :, px * 128 : px * 128 + 128] = hidden_grad[:, at : at + 128]
        return hidden_grad

    def split_out(out_low, og):
        mixed = dot(out_low, shuffle).astype(BF16)
        og[0] = mixed[:, 0:256]
        og[1] = mixed[:, 256:512]

    attend(0, kv_own.at[0], kv_own.at[1], begin=True)
    for name in ("dpos", "targets", "wup", "wdown", "whead"):
        loads[name].wait()
    ring_next(0, 0)
    part_rows = pl.ds(pl.multiple_of(seg * HALF, 16), HALF)
    stream_m = mtok_ref[...].astype(F32)[None, :] + dpos[part_rows, :].astype(F32)
    patch = iota((HALF, TILE), 0) + seg * HALF
    pick = (iota((HALF, TILE), 1) == patch).astype(F32).astype(BF16)
    goal_m = dot_nt(pick, targets[...])
    keep_m = 1.0 - seen_col[part_rows, :][:, 0:1]
    masked = []

    def ready_m():
        masked.append(send("unit_m", unit_m, unit_ms, sibling))
        masked.append(send("act_m", act_m, act_ms, sibling))
        ring_next(1, 0)

    normal, inverse, slope, out_grad = decode_forward(
        stream_m, goal_m, keep_m, unit_m, act_m, ready_m
    )
    attend(2 * ROWS, kv_r.at[0, 0], kv_l.at[0, 0])
    ring_next(0, 1)
    out_low = out_grad.astype(BF16)
    split_out(out_low, og_m)
    masked.append(send("og_m", og_m.at[1 - core], og_ms, sibling))
    decode_hidden(out_low, slope, hg_m)
    masked.append(send("hg_m", hg_m.at[1 - core], hg_ms, sibling))
    attend(4 * ROWS, kv_r.at[1, 0], kv_l.at[1, 0])
    ring_next(1, 1)
    attend(6 * ROWS, kv_r.at[0, 1], kv_l.at[0, 1])
    slot_first = pl.multiple_of(seg * SEG_STEP, 16)
    slot_rows = pl.ds(slot_first, SLOTS)
    chosen_part = selector[slot_rows, :]
    pos_slot[...] = dot(chosen_part, dpos[...])
    tgt_slot[...] = dot_nt(chosen_part, targets[...])
    number = iota((SLOTS, 128), 0) + seg * SEG_STEP
    kept = (number.astype(F32) < count) & (number >= seg * SLOTS)
    mask_slot[...] = jnp.where(kept, 1.0, 0.0)
    ring_next(0, 2)
    attend(8 * ROWS, kv_r.at[1, 1], kv_l.at[1, 1])
    for copy in masked:
        copy.wait_recv()
    gd_acc[...] = dot_tn(og_m[core], act_m[...]) + dot_tn(og_ms[...], act_ms[...])
    ring_next(1, 2)
    attend(10 * ROWS, kv_r.at[0, 2], kv_l.at[0, 2])
    gu_acc[...] = dot_tn(unit_m[...], hg_m[core]) + dot_tn(unit_ms[...], hg_ms[...])
    attend(12 * ROWS, kv_r.at[1, 2], kv_l.at[1, 2])
    loads["wout"].wait()
    loads["wembed"].wait()
    for part in range(2):
        ring["r", part, 3, 0].wait_recv()
        ring["l", part, 3, 1].wait_recv()
    unfold(kv_d.at[0, 0], 14 * ROWS)
    unfold(kv_d.at[1, 0], 15 * ROWS)

    back = []
    for j in range(2):
        attend_head(j, 14 * ROWS)
        total = acc[j]
        done = (total * (1.0 / total[:, 80:81])).astype(BF16)
        att_out[j, 0] = done[0:ROWS]
        att_out[j, 1] = done[ROWS : 2 * ROWS]
        for step, i in ((2, 0), (1, 1), (-1, 1)):
            goal_seg = ((y + step + 4) % 4) // 2
            span = pl.ds(pl.multiple_of(goal_seg * SEG_STEP, 16), SLOTS)
            back.append(
                send("b%d%d" % (j, step + 4), att_out.at[j, i, span], att_in.at[y, j], at_y(step))
            )
        att_in[y, j] = att_out[j, 0, slot_rows, :]
    for copy in back:
        copy.wait_recv()
    pieces = [att_in[i // 2, i % 2][:, 0:80].astype(F32) for i in range(HEADS)]
    for c in range(2):
        att[c] = jnp.concatenate(pieces[c * 4 : c * 4 + 4], axis=1).astype(BF16)
    swap_att = send("att_s", att.at[1 - core], att_sib, sibling)
    attended = jnp.concatenate(pieces, axis=1).astype(BF16)

    encoded = packed[slot_rows, :].astype(F32) + dot(attended, wout[...])
    embedded = dot(encoded.astype(BF16), wembed[...])
    stream_v = embedded + pos_slot[...]
    swap = {}

    def ready_v():
        swap["unit"] = send("unit_v", unit_v, unit_vs, sibling)
        swap["act"] = send("act_v", act_v, act_vs, sibling)

    normal, inverse, slope, out_grad = decode_forward(
        stream_v, tgt_slot[...], mask_slot[:, 0:1], unit_v, act_v, ready_v
    )
    out_low = out_grad.astype(BF16)
    split_out(out_low, og_v)
    swap["og"] = send("og_v", og_v.at[1 - core], og_vs, sibling)
    hidden_grad = decode_hidden(out_low, slope, hg_v)
    swap["hg"] = send("hg_v", hg_v.at[1 - core], hg_vs, sibling)

    def direct_sum(name, chunks, landing, place, at):
        copies = [
            send(name + str(step), chunks.at[(place + step) % 4], landing.at[step - 1], at(step))
            for step in range(1, 4)
        ]

        def finish():
            total = chunks[place].astype(F32)
            for step in range(3):
                copies[step].wait_recv()
                total = total + landing[step].astype(F32)
            return total

        return finish

    swap["act"].wait_recv()
    swap["og"].wait_recv()
    gd_t = gd_acc[...] + dot_tn(og_v[core], act_v[...]) + dot_tn(og_vs[...], act_vs[...])
    gd_t = gd_t.astype(BF16)
    for py in range(4):
        for px in range(4):
            for k in range(4):
                r = (py // 2) * 128 + px * 32
                c = (py % 2) * 512 + k * 128
                at = px * 128 + k * 32
                rs_gd[py, at : at + 32, :] = gd_t[r : r + 32, c : c + 128]
    finish_gd = direct_sum("gd", rs_gd, in_gd, y, at_y)

    unit_grad = dot_nt(hidden_grad, wup[...])
    cross = jnp.mean(unit_grad * normal, axis=-1, keepdims=True)
    middle = jnp.mean(unit_grad, axis=-1, keepdims=True)
    stream_grad = out_grad + inverse * (unit_grad - middle - normal * cross)
    sg_v[...] = stream_grad.astype(BF16)
    swap["sg"] = send("sg_v", sg_v, sg_vs, sibling)

    swap["unit"].wait_recv()
    swap["hg"].wait_recv()
    gu_t = gu_acc[...] + dot_tn(unit_v[...], hg_v[core]) + dot_tn(unit_vs[...], hg_vs[...])
    gu_t = gu_t.astype(BF16)
    for px in range(4):
        rs_gu[px] = gu_t[:, px * 128 : px * 128 + 128]
    finish_gu = direct_sum("gu", rs_gu, in_gu, x, at_x)

    swap_att.wait_recv()
    swap["sg"].wait_recv()
    inner = dot_tn(att[core], sg_v[...]) + dot_tn(att_sib[...], sg_vs[...])
    inner = inner.astype(BF16)
    for p in range(4):
        rs_g[p] = inner[0:160, p * 128 : p * 128 + 128]
        rs_h[p] = inner[160:320, p * 128 : p * 128 + 128]
    finish_g = direct_sum("g", rs_g, in_g, x, at_x)
    finish_h = direct_sum("h", rs_h, in_h, y, at_y)

    g_1 = (finish_g(), finish_h())
    for pz in range(8):
        r = 40 * (pz % 4)
        piece = jnp.concatenate([g_1[pz // 4][r : r + 40], jnp.zeros((8, 128), F32)], axis=0)
        zg[pz] = piece.astype(BF16)
    row_copies = [
        send("zg%d" % step, zg.at[(z + step) % 8], zgr.at[step - 1], at_z(step))
        for step in range(1, 8)
    ]
    gd_1 = finish_gd()
    for px in range(4):
        rs_gd2[px] = gd_1[px * 128 : px * 128 + 128].astype(BF16)
    finish_gd2 = direct_sum("gd2", rs_gd2, in_gd2, x, at_x)
    gu_1 = finish_gu()
    lane128 = iota((128, 128), 1)
    for py in range(4):
        first = gu_1[(py % 2) * 256 : (py % 2) * 256 + 128]
        second = gu_1[(py % 2) * 256 + 128 : (py % 2) * 256 + 256]
        if py // 2 == 0:
            pair = jnp.where(lane128 < 64, first, pltpu.roll(second, 64, 1))
        else:
            pair = jnp.where(lane128 < 64, pltpu.roll(first, 64, 1), second)
        rs_gu2[py] = pair.astype(BF16)
    finish_gu2 = direct_sum("gu2", rs_gu2, in_gu2, y, at_y)
    total = zg[z].astype(F32)
    for step in range(1, 8):
        row_copies[step - 1].wait_recv()
        total = total + zgr[step - 1].astype(F32)
    ag[...] = total.astype(BF16)
    spread = []
    for px in range(4):
        for pc in range(2):
            for half in range(2):
                target = device((x + px) % 4, pc, core + 2 * half, z)
                away = None
                if px == 0:
                    away = (core != pc) | (y != core + 2 * half)
                slot = N_SEND + len(spread)
                copy = describe(ag, gr.at[y, x], target, slot, N_NAMED + y * 4 + x)
                if away is None:
                    copy.start()
                else:
                    pl.when(away)(copy.start)
                spread.append((copy, away))

    @pl.when(user)
    def _():
        gr[y, x] = ag[...]

    gd_2 = finish_gd2()
    gu_2 = finish_gu2()
    lane32 = iota((32, 128), 1)
    for pz in range(8):
        up = gu_2[(pz % 4) * 32 : (pz % 4) * 32 + 32]
        if pz // 4 == 1:
            up = pltpu.roll(up, 64, 1)
        down = gd_2[(pz // 2) * 32 : (pz // 2) * 32 + 32]
        if pz % 2 == 0:
            down = pltpu.roll(down, 64, 1)
        zs[pz] = jnp.where(lane32 < 64, up, down).astype(BF16)
    last = []
    for step in range(1, 8):
        last.append(send("z%d" % step, zs.at[(z + step) % 8], zr.at[step - 1], at_z(step)))

    result = zs[z].astype(F32)
    for step in range(1, 8):
        last[step - 1].wait_recv()
        result = result + zr[step - 1].astype(F32)
    sums_ref[0:32, :] = result
    for py in range(4):
        for px in range(4):
            landed = describe(ag, gr.at[py, px], sibling, 0, N_NAMED + py * 4 + px)
            here = user & (y == py) & (x == px)
            pl.when(jnp.logical_not(here))(landed.wait_recv)
    blocks = [[gr[py, px].astype(F32) for px in range(4)] for py in range(4)]
    by_x = jnp.concatenate([sum(blocks[py][p] for py in range(4)) for p in range(4)], axis=1)
    by_y = jnp.concatenate([sum(blocks[p][px] for px in range(4)) for p in range(4)], axis=1)
    rows_b = jnp.where(z < 4, by_x, by_y).astype(BF16)
    columns = pl.ds(pl.multiple_of((x * 4 + core * 2 + seg) * 80, 16), 80)
    sums_ref[32:72, 0:80] = dot_nt(rows_b, wembed[columns, :])[0:40]
    for copy, away in spread:
        if away is None:
            copy.wait_send()
        else:
            pl.when(away)(copy.wait_send)
    for copy in started[-N_SEND:]:
        copy.wait_send()


def split_sums(sums_ref, go_ref, gu_ref, gd_ref):
    go_ref[...] = sums_ref[32:72, 0:80]
    gu_ref[...] = sums_ref[0:32, 0:64]
    gd_ref[...] = pltpu.roll(sums_ref[0:32, :], 64, 1)[:, 0:64]


def on_device(
    tokens, targets, visible, w_qkv, w_out, w_embed, mask_token, dec_pos, w_up, w_down, w_head
):
    names.clear()
    anywhere = pl.BlockSpec(memory_space=pl.ANY)
    vmem = pl.BlockSpec(memory_space=pltpu.VMEM)

    def low(*shape):
        return pltpu.VMEM(shape, BF16)

    def wide(*shape):
        return pltpu.VMEM(shape, F32)

    scratch = [
        low(TILE, D), low(PIX, TILE), low(D, INNER), low(D, INNER), low(D, INNER), low(INNER, D),
        low(D, DEC), low(TILE, DEC), low(DEC, FF), low(FF, DEC), low(PIX, DEC),
        low(ROWS, TILE), wide(TILE, 128), low(ROWS, D), low(HEADS, ROWS, 256), low(2, ROWS, 256),
        low(2, PART, 128), low(2, 3, PART, 128), low(2, 3, PART, 128), low(2, 1, PART, 128),
        low(2, 16 * ROWS, 128), low(2, 16 * ROWS, 128), low(2, 2 * ROWS, 128),
        wide(2, 2 * ROWS, 128), wide(2, 2 * ROWS, 128),
        low(2, 2, ROWS, 128), low(4, 2, SLOTS, 128), low(2, SLOTS, 320), low(SLOTS, 320),
        wide(SLOTS, DEC), wide(SLOTS, PIX), wide(SLOTS, 128),
        low(HALF, DEC), low(HALF, FF), low(2, HALF, 256), low(2, HALF, DEC),
        low(HALF, DEC), low(HALF, FF), low(HALF, 256), low(HALF, DEC),
        wide(256, FF), wide(DEC, DEC),
        low(SLOTS, DEC), low(SLOTS, FF), low(2, SLOTS, 256), low(2, SLOTS, DEC), low(SLOTS, DEC),
        low(SLOTS, DEC), low(SLOTS, FF), low(SLOTS, 256), low(SLOTS, DEC), low(SLOTS, DEC),
        low(4, 512, 128), low(4, 512, 128), low(4, 160, 128), low(4, 160, 128), low(4, 128, 128), low(4, 128, 128),
        low(3, 512, 128), low(3, 512, 128), low(3, 160, 128), low(3, 160, 128), low(3, 128, 128), low(3, 128, 128),
        low(8, 32, 128), low(7, 32, 128), low(8, 48, 128), low(7, 48, 128), low(48, 128),
        low(4, 4, 48, 128),
        pltpu.SemaphoreType.DMA((N_SEND + 16,)),
        pltpu.SemaphoreType.DMA((N_NAMED + 16,)),
        pltpu.SemaphoreType.DMA((N_LOCAL,)),
    ]
    sums = pl.pallas_call(
        kernel,
        out_shape=jax.ShapeDtypeStruct((80, 128), F32),
        in_specs=[
            anywhere, anywhere, vmem, anywhere, anywhere, anywhere, vmem, anywhere, anywhere,
            anywhere, anywhere,
        ],
        out_specs=vmem,
        scratch_shapes=scratch,
        compiler_params=pltpu.CompilerParams(
            collective_id=0, has_side_effects=True, vmem_limit_bytes=56 * 1024 * 1024
        ),
    )(
        tokens[0], targets[0].T, visible, w_qkv, w_out, w_embed, mask_token, dec_pos, w_up,
        w_down, w_head.T,
    )
    grad_out, grad_up, grad_down = pl.pallas_call(
        split_sums,
        out_shape=(
            jax.ShapeDtypeStruct((40, 80), F32),
            jax.ShapeDtypeStruct((32, 64), F32),
            jax.ShapeDtypeStruct((32, 64), F32),
        ),
        in_specs=[vmem],
        out_specs=(vmem, vmem, vmem),
    )(sums)
    return grad_out, grad_up, grad_down.T


def solution(mesh):
    in_specs = (
        P("dp", "blk", None),
        P("dp", "blk", None),
        P("dp", "blk"),
        P(),
        P(),
        P(),
        P(),
        P("blk", None),
        P(),
        P(),
        P(),
    )
    out_specs = (
        P("blk", ("dp", "segment")),
        P("blk", ("dp", "segment")),
        P("blk", ("dp", "segment")),
    )
    return jax.shard_map(
        on_device, mesh=mesh, in_specs=in_specs, out_specs=out_specs, check_vma=False
    )
```

```python
import math

import jax
import jax.numpy as jnp
from jax import lax
from jax.experimental import pallas as pl
from jax.experimental.pallas import tpu as pltpu
from jax.sharding import PartitionSpec as P

MESH = pl.DeviceIdType.MESH
F32 = jnp.float32
BF16 = jnp.bfloat16

HEADS = 8
HEAD_DIM = 80
VIS_TILE = 96
TILE = 384
CAP = 168
ROWS = 176
D = 1280
DEC = 512
FF = 1024
PIX = 1176
INNER = 640
HALF = 192
SLOTS = 96
SEG_STEP = 80
PART = 448
EPS = 1e-05
OUT_MASK = -1e30


def dot(a, b):
    return lax.dot_general(a, b, (((1,), (0,)), ((), ())), preferred_element_type=F32)


def dot_nt(a, b):
    return lax.dot_general(a, b, (((1,), (1,)), ((), ())), preferred_element_type=F32)


def dot_tn(a, b):
    return lax.dot_general(a, b, (((0,), (0,)), ((), ())), preferred_element_type=F32)


def normalize(rows):
    center = rows - jnp.mean(rows, axis=-1, keepdims=True)
    inverse = lax.rsqrt(jnp.mean(center * center, axis=-1, keepdims=True) + EPS)
    return center * inverse, inverse


def iota(shape, axis):
    return lax.broadcasted_iota(jnp.int32, shape, axis)


names = []


def ident(name):
    if name not in names:
        names.append(name)
    return names.index(name)


N_SEND = 16
N_NAMED = 78
N_LOCAL = 13


def kernel(
    tokens_h, targets_h, vis_h, wqkv_h, wout_h, wembed_h, mtok_h, dpos_h, wup_h, wdown_h, whead_h,
    sums_ref,
    tokens, targets, wq, wk, wv, wout, wembed, dpos, wup, wdown, whead,
    selector, seen_col, packed, heads, other, kv_own, kv_r, kv_l, kv_d, keys, vals, qx, acc, top,
    att_out, att_in, att, att_sib, pos_slot, tgt_slot, mask_slot,
    unit_m, act_m, og_m, hg_m, unit_ms, act_ms, og_ms, hg_ms, gd_acc, gu_acc,
    unit_v, act_v, og_v, hg_v, sg_v, unit_vs, act_vs, og_vs, hg_vs, sg_vs,
    rs_gd, rs_gu, rs_g, rs_h, rs_gd2, rs_gu2,
    in_gd, in_gu, in_g, in_h, in_gd2, in_gu2,
    zs, zr, zg, zgr, ag, gr,
    vis_ref, mtok_ref, send_sem, recv_sem, load_sem,
):
    dp = lax.axis_index("dp")
    seg = lax.axis_index("segment")
    blk = lax.axis_index("blk")
    x, core = dp // 2, dp % 2
    y, z = seg * 2 + blk // 8, blk % 8
    y_lo = blk // 8

    def device(px, pc, py, pz):
        return (px * 2 + pc, py // 2, (py % 2) * 8 + pz)

    def at_x(step):
        return device((x + step + 4) % 4, core, y, z)

    def at_y(step):
        return device(x, core, (y + step + 4) % 4, z)

    def at_z(step):
        return device(x, core, y, (z + step + 8) % 8)

    sibling = device(x, 1 - core, y, z)

    loads = {}

    def load(name, src, dst):
        copy = pltpu.make_async_copy(src, dst, load_sem.at[len(loads)])
        copy.start()
        loads[name] = copy

    load("vis", vis_h, vis_ref)
    load("tokens", tokens_h, tokens)
    for name, dst, first in (("wk", wk, 640), ("wv", wv, 1280), ("wq", wq, 0)):
        load(name, wqkv_h.at[:, pl.ds(first, 640)], dst)

    barrier = pltpu.get_barrier_semaphore()
    user = core == y_lo
    peers = [sibling] + [at_z(step) for step in range(1, 8)]
    peers += [at_x(step) for step in range(1, 4)] + [at_y(step) for step in range(1, 4)]
    for peer in peers:
        pl.semaphore_signal(barrier, inc=1, device_id=peer, device_id_type=MESH)
    for px in range(4):
        for py in range(4):
            source = device((x + px) % 4, y_lo, (y + py) % 4, z)

            def greet():
                pl.semaphore_signal(barrier, inc=1, device_id=source, device_id_type=MESH)

            if px or py:
                greet()
            else:
                pl.when(jnp.logical_not(user))(greet)
    greetings = len(peers) + 16 - jnp.where(user, 1, 0)

    started = []

    def describe(src, dst, target, slot, name):
        return pltpu.make_async_remote_copy(
            src_ref=src,
            dst_ref=dst,
            send_sem=send_sem.at[slot],
            recv_sem=recv_sem.at[ident(name) if isinstance(name, str) else name],
            device_id=target,
            device_id_type=MESH,
        )

    def send(name, src, dst, target):
        count = len(started)
        if count >= N_SEND:
            started[count - N_SEND].wait_send()
        copy = describe(src, dst, target, count % N_SEND, name)
        copy.start()
        started.append(copy)
        return copy

    loads["vis"].wait()
    vis = vis_ref[...].astype(F32)
    tri = (iota((TILE, TILE), 0) <= iota((TILE, TILE), 1)).astype(F32).astype(BF16)
    vis8 = jnp.broadcast_to(vis, (8, TILE))
    position = dot(vis8.astype(BF16), tri)[0:1, :] - 1.0
    count = jnp.sum(vis, axis=1, keepdims=True)
    slot_ids = iota((ROWS, TILE), 0).astype(F32)
    chosen = jnp.where((position == slot_ids) & (vis > 0.5), 1.0, 0.0).astype(BF16)
    selector[...] = chosen
    loads["tokens"].wait()
    rows = dot(chosen, tokens[...])
    packed[...] = rows.astype(BF16)
    normed = normalize(rows)[0].astype(BF16)
    seen_col[...] = dot_tn(chosen, jnp.ones((ROWS, 128), BF16))
    projected = []
    for name, weight in (("wk", wk), ("wv", wv), ("wq", wq)):
        loads[name].wait()
        projected.append(dot(normed, weight[...]))
    slot_row = iota((ROWS, 256), 0)
    for h in range(HEADS):
        parts = [p[:, h * 80 : h * 80 + 80] for p in projected]
        block = jnp.concatenate(parts + [jnp.zeros((ROWS, 16), F32)], axis=1)
        block = jnp.where(slot_row >= CAP, count, block)
        heads[h] = block.astype(BF16)

    pl.semaphore_wait(barrier, greetings)
    up_head = ((y + 1) % 4) * 2
    down_head = ((y + 3) % 4) * 2 + 1
    from_down = send("qkv+", heads.at[up_head], other.at[0], at_y(1))
    from_up = send("qkv-", heads.at[down_head], other.at[1], at_y(-1))

    lane = iota((ROWS, 128), 1)
    slot128 = iota((ROWS, 128), 0).astype(F32)

    def make_query(block, j, first):
        window = pltpu.roll(block[:, 128:256].astype(F32), 96, 1)
        query = jnp.where(lane < 80, window, jnp.where(lane == 80, 1.0, 0.0))
        qx[j, first : first + ROWS, :] = query.astype(BF16)

    lane88 = iota((ROWS // 2, 128), 1)

    def fold(first, second, part):
        both = jnp.concatenate(
            [first[:, 0:160].astype(F32), second[:, 0:160].astype(F32), jnp.zeros((ROWS, 64), F32)],
            axis=1,
        )
        third = both[:, 256:384]
        third = jnp.where(lane88 < 64, third[0:88], pltpu.roll(third[88:ROWS], 64, 1))
        part[0:ROWS, :] = both[:, 0:128].astype(BF16)
        part[ROWS : 2 * ROWS, :] = both[:, 128:256].astype(BF16)
        third = jnp.concatenate([third, jnp.zeros((8, 128), F32)], axis=0)
        part[2 * ROWS : PART, :] = third.astype(BF16)

    def unfold(part, first):
        p0 = part[0:ROWS, :].astype(F32)
        p1 = part[ROWS : 2 * ROWS, :].astype(F32)
        third = part[2 * ROWS : PART, :].astype(F32)[0:88]
        p2 = jnp.concatenate([third, pltpu.roll(third, 64, 1)], axis=0)
        pairs = (
            (p0, pltpu.roll(jnp.concatenate([p0, p1], axis=1), 176, 1)),
            (pltpu.roll(p1, 96, 1), pltpu.roll(jnp.concatenate([p1, p2], axis=1), 144, 1)),
        )
        for j in range(2):
            key, value = pairs[j]
            counts = key[CAP : CAP + 1, :]
            outside = jnp.where((lane == 80) & (slot128 >= counts), OUT_MASK, 0.0)
            keys[j, first : first + ROWS, :] = jnp.where(lane < 80, key, outside).astype(BF16)
            vals[j, first : first + ROWS, :] = jnp.where(
                lane == 80, 1.0, value[:, 0:128]
            ).astype(BF16)

    ring = {}
    ring_halves = (pl.ds(0, PART // 2), pl.ds(PART // 2, PART // 2))

    def ring_send(way, part, step, half, src):
        buffer, to = (kv_r, 1) if way == "r" else (kv_l, -1)
        rows_of = ring_halves[half]
        ring[way, part, step, half] = send(
            "%s%d%d%d" % (way, step, part, half),
            src.at[rows_of],
            (buffer if step < 3 else kv_d).at[part, step % 3, rows_of],
            at_z(to),
        )

    def ring_start(part):
        for half in range(2):
            for way in "rl":
                ring_send(way, part, 0, half, kv_own.at[part])

    def ring_next(part, step):
        for half in range(2):
            for way, buffer in (("r", kv_r), ("l", kv_l)):
                ring[way, part, step, half].wait_recv()
                if step < 2 or (way == "r") == (half == 0):
                    ring_send(way, part, step + 1, half, buffer.at[part, step])

    own = [heads[y * 2], heads[y * 2 + 1]]
    fold(own[0], own[1], kv_own.at[0])
    ring_start(0)
    load("mtok", mtok_h, mtok_ref)
    load("dpos", dpos_h, dpos)
    load("targets", targets_h, targets)
    load("wup", wup_h, wup)
    load("wdown", wdown_h, wdown)
    load("whead", whead_h, whead)
    load("wout", wout_h, wout)
    load("wembed", wembed_h, wembed)
    for j in range(2):
        make_query(own[j], j, 0)
    from_down.wait_recv()
    from_up.wait_recv()
    others = [other[0], other[1]]
    fold(others[0], others[1], kv_own.at[1])
    ring_start(1)
    for j in range(2):
        make_query(others[j], j, ROWS)

    scale = math.log2(math.e) / math.sqrt(HEAD_DIM)

    def attend_head(j, first, begin=False):
        span = slice(first, first + 2 * ROWS)
        scores = dot_nt(qx[j], keys[j, span, :])
        best = jnp.max(scores, axis=1, keepdims=True)
        if not begin:
            before = top[j]
            best = jnp.maximum(before[:, 0:1], best)
        probs = jnp.exp2((scores - best) * scale).astype(BF16)
        term = dot(probs, vals[j, span, :])
        if not begin:
            term = term + acc[j] * jnp.exp2((before - best) * scale)
        acc[j] = term
        top[j] = jnp.broadcast_to(best, (2 * ROWS, 128))

    def attend(first, one, two, begin=False):
        unfold(one, first)
        unfold(two, first + ROWS)
        for j in range(2):
            attend_head(j, first, begin)

    grad_scale = 8.0 / math.sqrt(8 * 16 * (TILE - VIS_TILE))
    root_half = 1.0 / math.sqrt(2.0)
    order = iota((DEC, DEC), 1)
    source = (order // 32 % 4) * 128 + (order // 256) * 64 + (order // 128 % 2) * 32 + order % 32
    shuffle = (iota((DEC, DEC), 0) == source).astype(F32).astype(BF16)

    def decode_forward(stream, goal, keep, unit, act, ready):
        normal, inverse = normalize(stream)
        low = normal.astype(BF16)
        unit[...] = low
        hidden = dot(low, wup[...])
        cumulative = 0.5 * (1.0 + lax.erf(hidden * root_half))
        active = (hidden * cumulative).astype(BF16)
        act[...] = active
        ready()
        slope = cumulative + hidden * jnp.exp(-0.5 * hidden * hidden) * (
            1.0 / math.sqrt(2.0 * math.pi)
        )
        stream_out = stream + dot(active, wdown[...])
        predicted = dot_nt(stream_out.astype(BF16), whead[...])
        pred_grad = ((predicted - goal) * (keep * grad_scale)).astype(BF16)
        out_grad = dot(pred_grad, whead[...])
        return normal, inverse, slope, out_grad

    def decode_hidden(out_low, slope, hg):
        hidden_grad = (dot_nt(out_low, wdown[...]) * slope).astype(BF16)
        for c in range(2):
            for px in range(4):
                at = px * 256 + c * 128
                hg[c, :, px * 128 : px * 128 + 128] = hidden_grad[:, at : at + 128]
        return hidden_grad

    def split_out(out_low, og):
        mixed = dot(out_low, shuffle).astype(BF16)
        og[0] = mixed[:, 0:256]
        og[1] = mixed[:, 256:512]

    attend(0, kv_own.at[0], kv_own.at[1], begin=True)
    for name in ("mtok", "dpos", "targets", "wup", "wdown", "whead"):
        loads[name].wait()
    ring_next(0, 0)
    part_rows = pl.ds(pl.multiple_of(seg * HALF, 16), HALF)
    stream_m = mtok_ref[...].astype(F32)[None, :] + dpos[part_rows, :].astype(F32)
    patch = iota((HALF, TILE), 0) + seg * HALF
    pick = (iota((HALF, TILE), 1) == patch).astype(F32).astype(BF16)
    goal_m = dot_nt(pick, targets[...])
    keep_m = 1.0 - seen_col[part_rows, :][:, 0:1]
    masked = []

    def ready_m():
        masked.append(send("unit_m", unit_m, unit_ms, sibling))
        masked.append(send("act_m", act_m, act_ms, sibling))
        ring_next(1, 0)

    normal, inverse, slope, out_grad = decode_forward(
        stream_m, goal_m, keep_m, unit_m, act_m, ready_m
    )
    attend(2 * ROWS, kv_r.at[0, 0], kv_l.at[0, 0])
    ring_next(0, 1)
    out_low = out_grad.astype(BF16)
    split_out(out_low, og_m)
    masked.append(send("og_m", og_m.at[1 - core], og_ms, sibling))
    decode_hidden(out_low, slope, hg_m)
    masked.append(send("hg_m", hg_m.at[1 - core], hg_ms, sibling))
    attend(4 * ROWS, kv_r.at[1, 0], kv_l.at[1, 0])
    ring_next(1, 1)
    attend(6 * ROWS, kv_r.at[0, 1], kv_l.at[0, 1])
    slot_first = pl.multiple_of(seg * SEG_STEP, 16)
    slot_rows = pl.ds(slot_first, SLOTS)
    chosen_part = selector[slot_rows, :]
    pos_slot[...] = dot(chosen_part, dpos[...])
    tgt_slot[...] = dot_nt(chosen_part, targets[...])
    number = iota((SLOTS, 128), 0) + seg * SEG_STEP
    kept = (number.astype(F32) < count) & (number >= seg * SLOTS)
    mask_slot[...] = jnp.where(kept, 1.0, 0.0)
    ring_next(0, 2)
    attend(8 * ROWS, kv_r.at[1, 1], kv_l.at[1, 1])
    for copy in masked:
        copy.wait_recv()
    gd_acc[...] = dot_tn(og_m[core], act_m[...]) + dot_tn(og_ms[...], act_ms[...])
    ring_next(1, 2)
    attend(10 * ROWS, kv_r.at[0, 2], kv_l.at[0, 2])
    gu_acc[...] = dot_tn(unit_m[...], hg_m[core]) + dot_tn(unit_ms[...], hg_ms[...])
    attend(12 * ROWS, kv_r.at[1, 2], kv_l.at[1, 2])
    loads["wout"].wait()
    loads["wembed"].wait()
    for part in range(2):
        ring["r", part, 3, 0].wait_recv()
        ring["l", part, 3, 1].wait_recv()
    unfold(kv_d.at[0, 0], 14 * ROWS)
    unfold(kv_d.at[1, 0], 15 * ROWS)

    back = []
    for j in range(2):
        attend_head(j, 14 * ROWS)
        total = acc[j]
        done = (total * (1.0 / total[:, 80:81])).astype(BF16)
        att_out[j, 0] = done[0:ROWS]
        att_out[j, 1] = done[ROWS : 2 * ROWS]
        for step, i in ((2, 0), (1, 1), (-1, 1)):
            goal_seg = ((y + step + 4) % 4) // 2
            span = pl.ds(pl.multiple_of(goal_seg * SEG_STEP, 16), SLOTS)
            back.append(
                send("b%d%d" % (j, step + 4), att_out.at[j, i, span], att_in.at[y, j], at_y(step))
            )
        att_in[y, j] = att_out[j, 0, slot_rows, :]
    for copy in back:
        copy.wait_recv()
    pieces = [att_in[i // 2, i % 2][:, 0:80].astype(F32) for i in range(HEADS)]
    for c in range(2):
        att[c] = jnp.concatenate(pieces[c * 4 : c * 4 + 4], axis=1).astype(BF16)
    swap_att = send("att_s", att.at[1 - core], att_sib, sibling)
    attended = jnp.concatenate(pieces, axis=1).astype(BF16)

    encoded = packed[slot_rows, :].astype(F32) + dot(attended, wout[...])
    embedded = dot(encoded.astype(BF16), wembed[...])
    stream_v = embedded + pos_slot[...]
    swap = {}

    def ready_v():
        swap["unit"] = send("unit_v", unit_v, unit_vs, sibling)
        swap["act"] = send("act_v", act_v, act_vs, sibling)

    normal, inverse, slope, out_grad = decode_forward(
        stream_v, tgt_slot[...], mask_slot[:, 0:1], unit_v, act_v, ready_v
    )
    out_low = out_grad.astype(BF16)
    split_out(out_low, og_v)
    swap["og"] = send("og_v", og_v.at[1 - core], og_vs, sibling)
    hidden_grad = decode_hidden(out_low, slope, hg_v)
    swap["hg"] = send("hg_v", hg_v.at[1 - core], hg_vs, sibling)

    def direct_sum(name, chunks, landing, place, at):
        copies = [
            send(name + str(step), chunks.at[(place + step) % 4], landing.at[step - 1], at(step))
            for step in range(1, 4)
        ]

        def finish():
            total = chunks[place].astype(F32)
            for step in range(3):
                copies[step].wait_recv()
                total = total + landing[step].astype(F32)
            return total

        return finish

    swap["act"].wait_recv()
    swap["og"].wait_recv()
    gd_t = gd_acc[...] + dot_tn(og_v[core], act_v[...]) + dot_tn(og_vs[...], act_vs[...])
    gd_t = gd_t.astype(BF16)
    for py in range(4):
        for px in range(4):
            for k in range(4):
                r = (py // 2) * 128 + px * 32
                c = (py % 2) * 512 + k * 128
                at = px * 128 + k * 32
                rs_gd[py, at : at + 32, :] = gd_t[r : r + 32, c : c + 128]
    finish_gd = direct_sum("gd", rs_gd, in_gd, y, at_y)

    unit_grad = dot_nt(hidden_grad, wup[...])
    cross = jnp.mean(unit_grad * normal, axis=-1, keepdims=True)
    middle = jnp.mean(unit_grad, axis=-1, keepdims=True)
    stream_grad = out_grad + inverse * (unit_grad - middle - normal * cross)
    sg_v[...] = stream_grad.astype(BF16)
    swap["sg"] = send("sg_v", sg_v, sg_vs, sibling)

    swap["unit"].wait_recv()
    swap["hg"].wait_recv()
    gu_t = gu_acc[...] + dot_tn(unit_v[...], hg_v[core]) + dot_tn(unit_vs[...], hg_vs[...])
    gu_t = gu_t.astype(BF16)
    for px in range(4):
        rs_gu[px] = gu_t[:, px * 128 : px * 128 + 128]
    finish_gu = direct_sum("gu", rs_gu, in_gu, x, at_x)

    swap_att.wait_recv()
    swap["sg"].wait_recv()
    inner = dot_tn(att[core], sg_v[...]) + dot_tn(att_sib[...], sg_vs[...])
    inner = inner.astype(BF16)
    for p in range(4):
        rs_g[p] = inner[0:160, p * 128 : p * 128 + 128]
        rs_h[p] = inner[160:320, p * 128 : p * 128 + 128]
    finish_g = direct_sum("g", rs_g, in_g, x, at_x)
    finish_h = direct_sum("h", rs_h, in_h, y, at_y)

    g_1 = (finish_g(), finish_h())
    for pz in range(8):
        r = 40 * (pz % 4)
        piece = jnp.concatenate([g_1[pz // 4][r : r + 40], jnp.zeros((8, 128), F32)], axis=0)
        zg[pz] = piece.astype(BF16)
    row_copies = [
        send("zg%d" % step, zg.at[(z + step) % 8], zgr.at[step - 1], at_z(step))
        for step in range(1, 8)
    ]
    gd_1 = finish_gd()
    for px in range(4):
        rs_gd2[px] = gd_1[px * 128 : px * 128 + 128].astype(BF16)
    finish_gd2 = direct_sum("gd2", rs_gd2, in_gd2, x, at_x)
    gu_1 = finish_gu()
    lane128 = iota((128, 128), 1)
    for py in range(4):
        first = gu_1[(py % 2) * 256 : (py % 2) * 256 + 128]
        second = gu_1[(py % 2) * 256 + 128 : (py % 2) * 256 + 256]
        if py // 2 == 0:
            pair = jnp.where(lane128 < 64, first, pltpu.roll(second, 64, 1))
        else:
            pair = jnp.where(lane128 < 64, pltpu.roll(first, 64, 1), second)
        rs_gu2[py] = pair.astype(BF16)
    finish_gu2 = direct_sum("gu2", rs_gu2, in_gu2, y, at_y)
    total = zg[z].astype(F32)
    for step in range(1, 8):
        row_copies[step - 1].wait_recv()
        total = total + zgr[step - 1].astype(F32)
    ag[...] = total.astype(BF16)
    spread = []
    for px in range(4):
        for pc in range(2):
            for half in range(2):
                target = device((x + px) % 4, pc, core + 2 * half, z)
                away = None
                if px == 0:
                    away = (core != pc) | (y != core + 2 * half)
                slot = N_SEND + len(spread)
                copy = describe(ag, gr.at[y, x], target, slot, N_NAMED + y * 4 + x)
                if away is None:
                    copy.start()
                else:
                    pl.when(away)(copy.start)
                spread.append((copy, away))

    @pl.when(user)
    def _():
        gr[y, x] = ag[...]

    gd_2 = finish_gd2()
    gu_2 = finish_gu2()
    lane32 = iota((32, 128), 1)
    for pz in range(8):
        up = gu_2[(pz % 4) * 32 : (pz % 4) * 32 + 32]
        if pz // 4 == 1:
            up = pltpu.roll(up, 64, 1)
        down = gd_2[(pz // 2) * 32 : (pz // 2) * 32 + 32]
        if pz % 2 == 0:
            down = pltpu.roll(down, 64, 1)
        zs[pz] = jnp.where(lane32 < 64, up, down).astype(BF16)
    last = []
    for step in range(1, 8):
        last.append(send("z%d" % step, zs.at[(z + step) % 8], zr.at[step - 1], at_z(step)))

    result = zs[z].astype(F32)
    for step in range(1, 8):
        last[step - 1].wait_recv()
        result = result + zr[step - 1].astype(F32)
    sums_ref[0:32, :] = result
    for py in range(4):
        for px in range(4):
            landed = describe(ag, gr.at[py, px], sibling, 0, N_NAMED + py * 4 + px)
            here = user & (y == py) & (x == px)
            pl.when(jnp.logical_not(here))(landed.wait_recv)
    blocks = [[gr[py, px].astype(F32) for px in range(4)] for py in range(4)]
    by_x = jnp.concatenate([sum(blocks[py][p] for py in range(4)) for p in range(4)], axis=1)
    by_y = jnp.concatenate([sum(blocks[p][px] for px in range(4)) for p in range(4)], axis=1)
    rows_b = jnp.where(z < 4, by_x, by_y).astype(BF16)
    columns = pl.ds(pl.multiple_of((x * 4 + core * 2 + seg) * 80, 16), 80)
    sums_ref[32:72, 0:80] = dot_nt(rows_b, wembed[columns, :])[0:40]
    for copy, away in spread:
        if away is None:
            copy.wait_send()
        else:
            pl.when(away)(copy.wait_send)
    for copy in started[-N_SEND:]:
        copy.wait_send()


def split_sums(sums_ref, go_ref, gu_ref, gd_ref):
    go_ref[...] = sums_ref[32:72, 0:80]
    gu_ref[...] = sums_ref[0:32, 0:64]
    gd_ref[...] = pltpu.roll(sums_ref[0:32, :], 64, 1)[:, 0:64]


def on_device(
    tokens, targets, visible, w_qkv, w_out, w_embed, mask_token, dec_pos, w_up, w_down, w_head
):
    names.clear()
    anywhere = pl.BlockSpec(memory_space=pl.ANY)
    vmem = pl.BlockSpec(memory_space=pltpu.VMEM)

    def low(*shape):
        return pltpu.VMEM(shape, BF16)

    def wide(*shape):
        return pltpu.VMEM(shape, F32)

    scratch = [
        low(TILE, D), low(PIX, TILE), low(D, INNER), low(D, INNER), low(D, INNER), low(INNER, D),
        low(D, DEC), low(TILE, DEC), low(DEC, FF), low(FF, DEC), low(PIX, DEC),
        low(ROWS, TILE), wide(TILE, 128), low(ROWS, D), low(HEADS, ROWS, 256), low(2, ROWS, 256),
        low(2, PART, 128), low(2, 3, PART, 128), low(2, 3, PART, 128), low(2, 1, PART, 128),
        low(2, 16 * ROWS, 128), low(2, 16 * ROWS, 128), low(2, 2 * ROWS, 128),
        wide(2, 2 * ROWS, 128), wide(2, 2 * ROWS, 128),
        low(2, 2, ROWS, 128), low(4, 2, SLOTS, 128), low(2, SLOTS, 320), low(SLOTS, 320),
        wide(SLOTS, DEC), wide(SLOTS, PIX), wide(SLOTS, 128),
        low(HALF, DEC), low(HALF, FF), low(2, HALF, 256), low(2, HALF, DEC),
        low(HALF, DEC), low(HALF, FF), low(HALF, 256), low(HALF, DEC),
        wide(256, FF), wide(DEC, DEC),
        low(SLOTS, DEC), low(SLOTS, FF), low(2, SLOTS, 256), low(2, SLOTS, DEC), low(SLOTS, DEC),
        low(SLOTS, DEC), low(SLOTS, FF), low(SLOTS, 256), low(SLOTS, DEC), low(SLOTS, DEC),
        low(4, 512, 128), low(4, 512, 128), low(4, 160, 128), low(4, 160, 128), low(4, 128, 128), low(4, 128, 128),
        low(3, 512, 128), low(3, 512, 128), low(3, 160, 128), low(3, 160, 128), low(3, 128, 128), low(3, 128, 128),
        low(8, 32, 128), low(7, 32, 128), low(8, 48, 128), low(7, 48, 128), low(48, 128),
        low(4, 4, 48, 128),
        pltpu.VMEM((1, TILE), jnp.int32), low(DEC),
        pltpu.SemaphoreType.DMA((N_SEND + 16,)),
        pltpu.SemaphoreType.DMA((N_NAMED + 16,)),
        pltpu.SemaphoreType.DMA((N_LOCAL,)),
    ]
    sums = pl.pallas_call(
        kernel,
        out_shape=jax.ShapeDtypeStruct((80, 128), F32),
        in_specs=[
            anywhere, anywhere, anywhere, anywhere, anywhere, anywhere, anywhere, anywhere, anywhere,
            anywhere, anywhere,
        ],
        out_specs=vmem,
        scratch_shapes=scratch,
        compiler_params=pltpu.CompilerParams(
            collective_id=0, has_side_effects=True, vmem_limit_bytes=56 * 1024 * 1024
        ),
    )(
        tokens[0], targets[0].T, visible, w_qkv, w_out, w_embed, mask_token, dec_pos, w_up,
        w_down, w_head.T,
    )
    grad_out, grad_up, grad_down = pl.pallas_call(
        split_sums,
        out_shape=(
            jax.ShapeDtypeStruct((40, 80), F32),
            jax.ShapeDtypeStruct((32, 64), F32),
            jax.ShapeDtypeStruct((32, 64), F32),
        ),
        in_specs=[vmem],
        out_specs=(vmem, vmem, vmem),
    )(sums)
    return grad_out, grad_up, grad_down.T


def solution(mesh):
    in_specs = (
        P("dp", "blk", None),
        P("dp", "blk", None),
        P("dp", "blk"),
        P(),
        P(),
        P(),
        P(),
        P("blk", None),
        P(),
        P(),
        P(),
    )
    out_specs = (
        P("blk", ("dp", "segment")),
        P("blk", ("dp", "segment")),
        P("blk", ("dp", "segment")),
    )
    return jax.shard_map(
        on_device, mesh=mesh, in_specs=in_specs, out_specs=out_specs, check_vma=False
    )
```
